128 devices in a mesh: dp: 64 (over x_hi, z, y, core), feat: 2 (over x_lo).
Axes of the slice: x: 4 (x_hi: 2, x_lo: 2; x = x_hi * 2 + x_lo), y: 4, z: 4, core: 2. Of those that a mesh axis runs over, the one named last changes fastest.
Arguments:
- image_emb: bfloat16 [65536, 1152], P('dp', 'feat'), may hold values from -6 to 6
- text_emb: bfloat16 [65536, 1152], P('dp', 'feat'), may hold values from -6 to 6
- image_ids: int32 [65536], P('dp'), may hold values from 0 to 63
- text_ids: int32 [65536], P('dp'), may hold values from 0 to 63
Outputs:
- row_loss: float32 [65536], P('dp')
- grad_image: float32 [65536, 1152], P('dp', 'feat')
- grad_text: float32 [65536, 1152], P('dp', 'feat')
The draws below stay inside these ranges and needn't reach their ends.
All inputs are finite; a program needn't handle non-finite values.
Results may differ from the reference program's by a relative error of at most 0.0018.
Values may be sent and summed in bfloat16 or wider, within the bound.
A program may use at most 128 MiB of HBM per device.

```python
import math
import jax
import jax.numpy as jnp
from jax import lax

D = 1152
TOK_DEV = 1024
HOPS = 2
ID_RANGE = 64
TOKENS = 65536
N_DP = 64


def with_ends(drawn, stream_key, low, top_value):
    shape = drawn.shape
    index_at = [jax.random.randint(jax.random.fold_in(stream_key, axis), (), 0, shape[axis]) for axis in range(len(shape))]
    drawn = drawn.at[tuple(index_at)].set(low)
    longest = shape.index(max(shape))
    index_at[longest] = (index_at[longest] + 1) % shape[longest]
    return drawn.at[tuple(index_at)].set(top_value)


def block_scale(rng, extent, cuts, low, top_value):
    level, own = 1.0, jax.random.fold_in(rng, 6)
    for dim, parts in cuts:
        steps = jnp.exp(jax.random.uniform(jax.random.fold_in(own, dim), (parts,), jnp.float32, low / len(cuts), top_value / len(cuts)))
        level = level * jnp.repeat(steps, extent[dim] // parts).reshape([-1 if axis == dim else 1 for axis in range(len(extent))])
    return level


def gaussian(key, dims, scale, reach, split=(), kind=jnp.bfloat16):
    factor_of = block_scale(key, dims, split, -0.22, 0.18) if split else 1.0
    array = jax.random.normal(key, dims, jnp.float32) * scale * factor_of
    return jnp.minimum(jnp.maximum(array, -reach), reach).astype(kind)


def setup_inputs(seed: int = 0) -> dict:
    seeds = jax.random.split(jax.random.key(seed), 5)
    return {
        "image_emb": gaussian(seeds[0], (TOKENS, D), 1.0, 6.0, ((0, 64), (1, 2))),
        "text_emb": gaussian(seeds[1], (TOKENS, D), 1.0, 6.0, ((0, 64), (1, 2))),
        "image_ids": with_ends(jax.random.randint(seeds[2], (TOKENS,), 0, ID_RANGE), jax.random.fold_in(seeds[2], 1), 0, ID_RANGE - 1).astype(jnp.int32),
        "text_ids": with_ends(jax.random.randint(seeds[3], (TOKENS,), 0, ID_RANGE), jax.random.fold_in(seeds[3], 1), 0, ID_RANGE - 1).astype(jnp.int32),
    }


logit_temper = 3.0
logit_bias = -4.0

def reference(image_emb, text_emb, image_ids, text_ids):
    blocks = N_DP
    tok_rows = TOK_DEV
    logit_scale = logit_temper / math.sqrt(D)
    images = image_emb.reshape(blocks, tok_rows, D).astype(jnp.float32)
    own_ids = image_ids.reshape(blocks, tok_rows)
    grad_image = jnp.zeros((blocks, tok_rows, D), jnp.float32)
    grad_text = jnp.zeros((blocks, tok_rows, D), jnp.float32)
    row_loss = jnp.zeros((blocks, tok_rows), jnp.float32)
    for hop_index in range(HOPS + 1):
        text_panel = jnp.roll(text_emb, hop_index * tok_rows, axis=0).reshape(blocks, tok_rows, D).astype(jnp.float32)
        panel_ids = jnp.roll(text_ids, hop_index * tok_rows).reshape(blocks, tok_rows)
        scores = jnp.einsum('ntd,nsd->nts', images, text_panel)
        logits = logit_scale * scores + logit_bias
        pair_sign = jnp.where(own_ids[:, :, None] == panel_ids[:, None, :], 1.0, -1.0).astype(jnp.float32)
        row_loss = row_loss + lax.optimization_barrier(jnp.sum(jax.nn.softplus(-pair_sign * logits), axis=2))
        weights = (-pair_sign * jax.nn.sigmoid(-pair_sign * logits)).astype(jnp.bfloat16).astype(jnp.float32)
        grad_image = grad_image + logit_scale * jnp.einsum('nts,nsd->ntd', weights, text_panel)
        contrib = logit_scale * jnp.einsum('nts,ntd->nsd', weights, images)
        grad_text = grad_text + jnp.roll(contrib, -hop_index, axis=0)
    row_loss = row_loss / float((HOPS + 1) * tok_rows)
    return (row_loss.reshape(blocks * tok_rows), grad_image.reshape(blocks * tok_rows, D), grad_text.reshape(blocks * tok_rows, D))
```

```python
import functools
import math

import jax
import jax.numpy as jnp
from jax import lax
from jax.experimental import pallas as pl
from jax.experimental.pallas import tpu as pltpu
from jax.sharding import PartitionSpec as P

HOPS = 2
MESH = pl.DeviceIdType.MESH
TEMPER = 3.0
BIAS = -4.0

F32 = jnp.float32
BF16 = jnp.bfloat16
LIFT = 2.0**48


def log1p_of(x):
    return jnp.where(x < 1e-3, x * (1.0 - 0.5 * x), jnp.log(1.0 + x))


def join(a, b):
    return a + b + a * b


def code(x):
    x = x * LIFT
    return (x * jnp.abs(x)).astype(BF16)


def decode(y):
    y = y.astype(F32)
    x = jnp.sqrt(jnp.abs(y)) * (1.0 / LIFT)
    return jnp.where(y < 0, -x, x)


def pack(tail):
    half = tail.shape[0] // 2
    return jnp.concatenate([tail[:half], tail[half:]], axis=1)


def unpack(packed):
    return jnp.concatenate([packed[:, :64], packed[:, 64:]], axis=0)


def kernel(
    n_dp, n_parts, scale, img, txt, iid, tid, loss_o, gi_o, gt_o,
    X, XTR, PK, IDS, VID, GV, GS, CS, CV, YS, YR, XS, XST, RX, RXT, PV, LS, LOS, LOR, LFIN,
    xs, xr, cs, cr, ys, yr, ids_s, ids_r, gs_s, gs_r, rs, rr, cvs, cvr, os, orr, los, lor,
):
    R = img.shape[0]
    H = R // 2
    C = R // n_parts
    NH = n_parts // 2
    MW = 512
    KW = X.shape[2]
    TL = 2 * MW
    d = lax.axis_index("dp")
    f = lax.axis_index("feat")
    n_cell = n_dp // 2
    c = d // 2
    a = lax.rem(d, 2)
    flip = c // (n_cell // 2)
    role = lax.rem(f + flip, 2)
    other = 1 - f
    c_next = lax.rem(c + 1, n_cell)
    c_last = lax.rem(c + n_cell - 1, n_cell)
    f_next = lax.rem(role + c_next // (n_cell // 2), 2)
    f_last = lax.rem(role + c_last // (n_cell // 2), 2)
    partner = (d, other)
    core = (2 * c + 1 - a, f)
    diag = (2 * c + 1 - a, other)

    def nxt(core_index):
        return (2 * c_next + core_index, f_next)

    def last(core_index):
        return (2 * c_last + core_index, f_last)

    own_cols = pl.ds(pl.multiple_of(f * MW, MW), MW)
    oth_cols = pl.ds(pl.multiple_of(other * MW, MW), MW)
    a_rows = pl.ds(pl.multiple_of(a * H, H), H)

    def chunk(j):
        return pl.ds(pl.multiple_of(j * C, C), C) if not isinstance(j, int) else pl.ds(j * C, C)

    def packed_chunk(j):
        half = C // 2
        return pl.ds(pl.multiple_of(j * half, half), half) if not isinstance(j, int) else pl.ds(j * half, half)

    def rcopy(src, dst, ssem, rsem, dev):
        return pltpu.make_async_remote_copy(
            src_ref=src, dst_ref=dst, send_sem=ssem, recv_sem=rsem, device_id=dev, device_id_type=MESH
        )

    def got(dst, rsem):
        pltpu.make_async_copy(dst, dst, rsem).wait()

    def sent(src, ssem):
        pltpu.make_async_copy(src, src, ssem).wait()

    barrier = pltpu.get_barrier_semaphore()
    peers = [partner, core, diag, nxt(0), nxt(1), last(0), last(1)]
    for dev in peers:
        pl.semaphore_signal(barrier, inc=1, device_id=dev, device_id_type=MESH)
    pl.semaphore_wait(barrier, len(peers))

    raws = (img, txt)

    def send_raw(kind, slot):
        raw = raws[kind]
        for j in range(n_parts):
            PK[kind, packed_chunk(j), :] = pack(raw[chunk(j), MW : MW + 64])
            rcopy(PK.at[kind, packed_chunk(j)], XTR.at[kind, packed_chunk(j)], xs.at[kind, 0, j], xr.at[kind, 0, j], partner).start()
            rcopy(raw.at[chunk(j), pl.ds(0, MW)], X.at[slot, chunk(j), own_cols], xs.at[kind, 1, j], xr.at[kind, 1, j], partner).start()

    def raw_sent(kind):
        for j in range(n_parts):
            sent(PK.at[kind, packed_chunk(j)], xs.at[kind, 0, j])
            sent(raws[kind].at[chunk(j), pl.ds(0, MW)], xs.at[kind, 1, j])

    def place(kind, slot):
        X[slot, :, own_cols] = raws[kind][:, 0:MW]

    def assemble(kind, slot, j):
        got(XTR.at[kind, packed_chunk(j)], xr.at[kind, 0, j])
        theirs = unpack(XTR[kind, packed_chunk(j), :])
        mine = raws[kind][chunk(j), MW : MW + 64]
        low, high = jnp.where(f == 0, mine, theirs), jnp.where(f == 0, theirs, mine)
        X[slot, chunk(j), TL:KW] = jnp.concatenate([low, high], axis=1)
        got(X.at[slot, chunk(j), oth_cols], xr.at[kind, 1, j])

    def whole(slot, j):
        return X.at[slot, chunk(j)]

    def to_core(slot, j):
        rcopy(whole(slot, j), whole(slot, j), cs.at[slot, j], cr.at[slot, j], core).start()

    def from_core(slot, j):
        got(whole(slot, j), cr.at[slot, j])

    def to_core_sent(slot, j):
        sent(whole(slot, j), cs.at[slot, j])

    def move(slot, j, dev):
        rcopy(whole(slot, j), whole(3, j), ys.at[j], yr.at[j], dev).start()

    def ids_to_core(slot):
        rcopy(IDS.at[slot], IDS.at[slot], ids_s.at[slot], ids_r.at[slot], core).start()

    def ids_move(slot, k, dev):
        rcopy(IDS.at[slot], IDS.at[3], ids_s.at[3 + k], ids_r.at[3], dev).start()

    def columns_of(v, slot):
        got(IDS.at[slot], ids_r.at[slot])
        column(v, slot)

    def column(v, slot):
        row = IDS[slot, 0:1, a_rows]
        VID[v] = jnp.transpose(jnp.broadcast_to(row, (128, H)))

    def unit(v, v_slot, s_slot, s_acc, j, image_rows):
        left = X[v_slot, a_rows, :]
        right = X[s_slot, chunk(j), :]
        scores = lax.dot_general(left, right, (((1,), (1,)), ((), ())), preferred_element_type=F32)
        logits = scale * scores + BIAS
        vid = VID[v]
        same = jnp.concatenate([vid] * (C // 128), axis=1) == IDS[s_slot, 0:1, chunk(j)]
        z = jnp.where(same, -logits, logits)
        e = jnp.exp(-jnp.abs(z))
        inv = 1.0 / (1.0 + e)
        sig = jnp.where(z >= 0, inv, e * inv)
        w = jnp.where(same, -sig, sig).astype(BF16)
        relu = jnp.maximum(z, 0.0)
        if image_rows:
            total, prod = relu[:, 0:128], e[:, 0:128]
            for t in range(1, C // 128):
                total = total + relu[:, t * 128 : (t + 1) * 128]
                prod = join(prod, e[:, t * 128 : (t + 1) * 128])
            PV[v, 0] += total
            PV[v, 1] = join(PV[v, 1], prod)
        else:
            total, prod = relu, e
            while total.shape[0] > 8:
                n = total.shape[0] // 2
                total = total[:n] + total[n:]
                prod = join(prod[:n], prod[n:])
            LS[:, chunk(j)] += total + log1p_of(prod)
        GV[v] += jnp.dot(w, right, preferred_element_type=F32)
        GS[s_acc, chunk(j), :] += lax.dot_general(w, left, (((0,), (0,)), ((), ())), preferred_element_type=F32)

    def tails(value):
        own = jnp.where(f == 0, value[:, 0:64], value[:, 64:128])
        oth = jnp.where(f == 0, value[:, 64:128], value[:, 0:64])
        return own, oth

    def give(b, k, main, tail, kind, dst, dev):
        XS[b, chunk(k), :] = code(scale * main)
        XST[b, packed_chunk(k), :] = pack(code(scale * tail))
        rcopy(XST.at[b, packed_chunk(k)], RXT.at[kind, packed_chunk(dst)], os.at[b, 0, k], orr.at[kind, 0, dst], dev).start()
        rcopy(XS.at[b, chunk(k)], RX.at[kind, chunk(dst)], os.at[b, 1, k], orr.at[kind, 1, dst], dev).start()

    def given(b, k):
        sent(XST.at[b, packed_chunk(k)], os.at[b, 0, k])
        sent(XS.at[b, chunk(k)], os.at[b, 1, k])

    def take(kind, j):
        got(RXT.at[kind, packed_chunk(j)], orr.at[kind, 0, j])
        got(RX.at[kind, chunk(j)], orr.at[kind, 1, j])
        return decode(RX[kind, chunk(j), :]), decode(unpack(RXT[kind, packed_chunk(j), :]))

    def keep(out, j, main, tail, scaled=False):
        out[chunk(j), 0:MW] = main if scaled else scale * main
        out[chunk(j), MW : MW + 64] = tail if scaled else scale * tail

    def keep_plus(out, kind, j):
        main, tail = take(kind, j)
        out[chunk(j), 0:MW] += main
        out[chunk(j), MW : MW + 64] += tail

    def turn_back(v, dev):
        for k in range(NH):
            YS[chunk(k), :] = code(GV[v, chunk(k), :])
            rcopy(YS.at[chunk(k)], YR.at[chunk(k)], rs.at[k], rr.at[k], dev).start()

    def turned_back():
        for k in range(NH):
            sent(YS.at[chunk(k)], rs.at[k])

    def v_chunk(v, k, returned):
        main_own, main_oth, tail = GV[v, chunk(k), own_cols], GV[v, chunk(k), oth_cols], GV[v, chunk(k), TL:KW]
        if returned:
            got(YR.at[chunk(k)], rr.at[k])
            main_own = main_own + decode(YR[chunk(k), own_cols])
            main_oth = main_oth + decode(YR[chunk(k), oth_cols])
            tail = tail + decode(YR[chunk(k), TL:KW])
        tail_own, tail_oth = tails(tail)
        return main_own, tail_own, main_oth, tail_oth

    def cv_send(k, main, tail):
        CV[0, chunk(k), 0:MW] = main
        CV[0, chunk(k), MW : MW + 128] = jnp.concatenate([tail, tail], axis=1)
        rcopy(CV.at[0, chunk(k)], CV.at[1, chunk(k)], cvs.at[k], cvr.at[k], core).start()

    def cv_take(k):
        got(CV.at[1, chunk(k)], cvr.at[k])
        return CV[1, chunk(k), 0:MW], CV[1, chunk(k), MW : MW + 64]

    def cv_sent():
        for k in range(NH):
            sent(CV.at[0, chunk(k)], cvs.at[k])

    def s_part(s_acc, j):
        rcopy(GS.at[s_acc, chunk(j)], CS.at[chunk(j)], gs_s.at[j], gs_r.at[j], core).start()

    def s_part_sent(s_acc):
        for j in range(n_parts):
            sent(GS.at[s_acc, chunk(j)], gs_s.at[j])

    def s_home(s_acc, j, out, b, kind, dev):
        got(CS.at[chunk(j)], gs_r.at[j])
        main_own = GS[s_acc, chunk(j), own_cols] + CS[chunk(j), own_cols]
        main_oth = GS[s_acc, chunk(j), oth_cols] + CS[chunk(j), oth_cols]
        tail_own, tail_oth = tails(GS[s_acc, chunk(j), TL:KW] + CS[chunk(j), TL:KW])
        give(b, j, main_oth, tail_oth, kind, j, dev)
        keep(out, j, main_own, tail_own)

    def zero():
        GV[...] = jnp.zeros_like(GV)
        GS[...] = jnp.zeros_like(GS)
        PV[...] = jnp.zeros_like(PV)
        LS[...] = jnp.zeros_like(LS)

    def row_of(v):
        col = PV[v, 0] + log1p_of(PV[v, 1])
        row = jnp.sum(jnp.transpose(col), axis=0, keepdims=True)
        return jnp.broadcast_to(row, (8, H))

    mean = 1.0 / float((HOPS + 1) * R)

    def loss_out():
        loss_o[...] = LFIN[...] * mean

    def loss_to_partner():
        rcopy(LFIN, LFIN, los.at[3], lor.at[3], partner).start()

    def role_0():
        @pl.when(a == 0)
        def _():
            send_raw(1, 1)
            IDS[0] = iid[...]
            IDS[1] = tid[...]
            ids_to_core(0)
            ids_to_core(1)
            ids_move(0, 0, last(0))
            ids_move(0, 1, last(1))
            place(0, 0)
            place(1, 1)

        @pl.when(a == 1)
        def _():
            send_raw(1, 2)
            send_raw(0, 0)
            IDS[2] = tid[...]
            ids_to_core(2)
            place(1, 2)

        zero()

        @pl.when(a == 0)
        def _():
            got(IDS.at[2], ids_r.at[2])
            columns_of(1, 3)
            column(0, 0)
            for j in range(n_parts):
                assemble(0, 0, j)
                if j >= NH:
                    to_core(0, j)
                move(0, j, last(j // NH))

        @pl.when(a == 1)
        def _():
            got(IDS.at[1], ids_r.at[1])
            columns_of(1, 3)
            columns_of(0, 0)
            for j in range(n_parts):
                assemble(1, 2, j)
                to_core(2, j)

        for k in range(NH):
            got(whole(3, a * NH + k), yr.at[a * NH + k])

        def first(j, carry):
            pl.when(a == 0)(lambda: from_core(2, j))
            unit(1, 3, 2, 0, j, True)
            pl.when(a == 0)(lambda: s_part(0, j))

            @pl.when((a == 1) & (j > 0))
            def _():
                s_home(0, j - 1, gt_o, 1, 1, partner)

            return carry

        lax.fori_loop(0, n_parts, first, 0)

        @pl.when(a == 1)
        def _():
            s_home(0, n_parts - 1, gt_o, 1, 1, partner)
            for j in range(NH, n_parts):
                from_core(0, j)

        def second(j, carry):
            @pl.when(a == 0)
            def _():
                assemble(1, 1, j)
                to_core(1, j)

            pl.when(a == 1)(lambda: from_core(1, j))
            unit(0, 0, 1, 1, j, True)
            unit(1, 3, 1, 1, j, True)
            pl.when(a == 1)(lambda: s_part(1, j))

            @pl.when((a == 0) & (j > 0))
            def _():
                s_home(1, j - 1, gt_o, 1, 1, partner)

            return carry

        lax.fori_loop(0, n_parts, second, 0)
        turn_back(1, nxt(a))

        LOS[0] = row_of(0)
        LOS[1] = row_of(1)
        rcopy(LOS.at[1], LOR.at[1 + a], los.at[1], lor.at[1 + a], nxt(0)).start()

        @pl.when(a == 1)
        def _():
            rcopy(LOS.at[0], LOR.at[0], los.at[0], lor.at[0], core).start()

        @pl.when(a == 0)
        def _():
            s_home(1, n_parts - 1, gt_o, 1, 1, partner)
            for i in range(3):
                got(LOR.at[i], lor.at[i])
            LFIN[:, 0:H] = LOS[0] + LOR[1]
            LFIN[:, H:R] = LOR[0] + LOR[2]
            loss_to_partner()
            loss_out()
            for k in range(NH):
                main, tail, main_oth, tail_oth = v_chunk(0, k, True)
                give(0, k, main_oth, tail_oth, 0, k, partner)
                keep(gi_o, k, main, tail)
            for j in range(n_parts):
                keep_plus(gt_o, 1, j)
            for k in range(NH):
                main, tail = cv_take(k)
                keep(gi_o, NH + k, main, tail)
            raw_sent(1)
            for j in range(n_parts):
                to_core_sent(1, j)
                sent(whole(0, j), ys.at[j])
            for j in range(NH, n_parts):
                to_core_sent(0, j)
            for k in (0, 1, 3, 4):
                sent(IDS.at[0], ids_s.at[k])
            s_part_sent(0)
            sent(LFIN, los.at[3])

        @pl.when(a == 1)
        def _():
            for k in range(NH):
                main, tail, main_oth, tail_oth = v_chunk(0, k, True)
                give(0, k, main_oth, tail_oth, 0, NH + k, diag)
                cv_send(k, main, tail)
            for j in range(n_parts):
                keep_plus(gt_o, 1, j)
            for j in range(n_parts):
                main, tail = take(0, j)
                keep(gi_o, j, main, tail, True)
            got(LFIN, lor.at[3])
            loss_out()
            raw_sent(0)
            raw_sent(1)
            for j in range(n_parts):
                to_core_sent(2, j)
            sent(IDS.at[2], ids_s.at[2])
            s_part_sent(1)
            sent(LOS.at[0], los.at[0])
            cv_sent()

        for k in range(NH):
            given(0, k)
        for j in range(n_parts):
            given(1, j)
        sent(LOS.at[1], los.at[1])
        turned_back()

    def role_1():
        @pl.when(a == 0)
        def _():
            send_raw(0, 0)
            send_raw(1, 1)
            IDS[1] = tid[...]
            ids_to_core(1)
            place(1, 1)

        @pl.when(a == 1)
        def _():
            send_raw(1, 2)
            IDS[0] = iid[...]
            IDS[2] = tid[...]
            ids_to_core(0)
            ids_to_core(2)
            ids_move(2, 0, nxt(0))
            ids_move(2, 1, nxt(1))
            place(1, 2)
            place(0, 0)

        zero()

        @pl.when(a == 0)
        def _():
            got(IDS.at[0], ids_r.at[0])
            columns_of(0, 2)
            columns_of(2, 3)
            column(1, 1)
            for j in range(n_parts):
                assemble(1, 1, j)
                if j >= NH:
                    to_core(1, j)
            for j in range(NH):
                from_core(2, j)

        @pl.when(a == 1)
        def _():
            columns_of(1, 1)
            columns_of(2, 3)
            column(0, 2)
            for j in range(n_parts):
                assemble(1, 2, j)
                if j < NH:
                    to_core(2, j)
                move(2, j, nxt(j // NH))
            for j in range(NH, n_parts):
                from_core(1, j)

        for k in range(NH):
            got(whole(3, a * NH + k), yr.at[a * NH + k])

        def step(j, carry):
            @pl.when(a == 1)
            def _():
                assemble(0, 0, j)
                to_core(0, j)

            pl.when(a == 0)(lambda: from_core(0, j))
            unit(0, 2, 0, 0, j, False)
            unit(1, 1, 0, 0, j, False)
            unit(2, 3, 0, 0, j, False)
            pl.when(a == 0)(lambda: s_part(0, j))

            @pl.when((a == 1) & (j > 0))
            def _():
                s_home(0, j - 1, gi_o, 2, 0, partner)

            return carry

        lax.fori_loop(0, n_parts, step, 0)
        turn_back(2, last(a))

        @pl.when(a == 0)
        def _():
            LOS[0] = LS[:, 0:H]
            LOS[1] = LS[:, H:R]
            for i in range(2):
                rcopy(LOS.at[i], LOR.at[i], los.at[i], lor.at[i], core).start()
            for k in range(NH):
                main, tail, main_oth, tail_oth = v_chunk(1, k, False)
                give(1, k, main_oth, tail_oth, 1, k, partner)
                keep(gt_o, k, main, tail)
            for k in range(NH):
                main, tail, main_oth, tail_oth = v_chunk(0, k, True)
                give(0, k, main_oth, tail_oth, 1, k, diag)
                cv_send(k, main, tail)
            for k in range(NH):
                main, tail = cv_take(k)
                keep(gt_o, NH + k, main, tail)
            for j in range(n_parts):
                keep_plus(gt_o, 1, j)
            for j in range(n_parts):
                main, tail = take(0, j)
                keep(gi_o, j, main, tail, True)
            got(LFIN, lor.at[3])
            loss_out()
            raw_sent(0)
            raw_sent(1)
            for j in range(NH, n_parts):
                to_core_sent(1, j)
            sent(IDS.at[1], ids_s.at[1])
            s_part_sent(0)
            for i in range(2):
                sent(LOS.at[i], los.at[i])

        @pl.when(a == 1)
        def _():
            s_home(0, n_parts - 1, gi_o, 2, 0, partner)
            for k in range(NH):
                main, tail, main_oth, tail_oth = v_chunk(1, k, False)
                give(1, k, main_oth, tail_oth, 1, NH + k, diag)
                cv_send(k, main, tail)
            for i in range(2):
                got(LOR.at[i], lor.at[i])
            sums = LS[...] + jnp.concatenate([LOR[0], LOR[1]], axis=1)
            LFIN[...] = jnp.broadcast_to(jnp.sum(sums, axis=0, keepdims=True), (8, R))
            loss_to_partner()
            loss_out()
            for k in range(NH):
                main, tail, main_oth, tail_oth = v_chunk(0, k, True)
                give(0, k, main_oth, tail_oth, 1, NH + k, partner)
                keep(gt_o, NH + k, main, tail)
            for k in range(NH):
                main, tail = cv_take(k)
                keep(gt_o, k, main, tail)
            for j in range(n_parts):
                keep_plus(gt_o, 1, j)
            raw_sent(1)
            for j in range(n_parts):
                to_core_sent(0, j)
                sent(whole(2, j), ys.at[j])
            for j in range(NH):
                to_core_sent(2, j)
            for k in (0, 2, 3, 4):
                sent(IDS.at[0], ids_s.at[k])
            for j in range(n_parts):
                given(2, j)
            sent(LFIN, los.at[3])

        for k in range(NH):
            given(0, k)
            given(1, k)
        turned_back()
        cv_sent()

    pl.when(role == 0)(role_0)
    pl.when(role == 1)(role_1)


def per_device(n_dp, n_parts, image_emb, text_emb, image_ids, text_ids):
    R, width = image_emb.shape
    H, C = R // 2, R // n_parts
    KW = 2 * width
    scale = TEMPER / math.sqrt(KW)
    ids = [jnp.broadcast_to(i[None, :], (8, R)) for i in (image_ids, text_ids)]
    dma = pltpu.SemaphoreType.DMA
    vmem = pltpu.VMEM
    scratch = [
        vmem((4, R, KW), BF16),
        vmem((2, R // 2, 128), BF16),
        vmem((2, R // 2, 128), BF16),
        vmem((4, 8, R), jnp.int32),
        vmem((3, H, 128), jnp.int32),
        vmem((3, H, KW), F32),
        vmem((2, R, KW), F32),
        vmem((R, KW), F32),
        vmem((2, H, 640), F32),
        vmem((H, KW), BF16),
        vmem((H, KW), BF16),
        vmem((3, R, 512), BF16),
        vmem((3, R // 2, 128), BF16),
        vmem((2, R, 512), BF16),
        vmem((2, R // 2, 128), BF16),
        vmem((3, 2, H, 128), F32),
        vmem((8, R), F32),
        vmem((2, 8, H), F32),
        vmem((3, 8, H), F32),
        vmem((8, R), F32),
        dma((2, 2, n_parts)), dma((2, 2, n_parts)),
        dma((3, n_parts)), dma((3, n_parts)),
        dma((n_parts,)), dma((n_parts,)),
        dma((5,)), dma((4,)),
        dma((n_parts,)), dma((n_parts,)),
        dma((n_parts,)), dma((n_parts,)),
        dma((n_parts,)), dma((n_parts,)),
        dma((3, 2, n_parts)), dma((2, 2, n_parts)),
        dma((4,)), dma((4,)),
    ]
    flops = 9 * 2 * H * R * KW
    loss, grad_image, grad_text = pl.pallas_call(
        functools.partial(kernel, n_dp, n_parts, scale),
        out_shape=[
            jax.ShapeDtypeStruct((8, R), F32),
            jax.ShapeDtypeStruct((R, width), F32),
            jax.ShapeDtypeStruct((R, width), F32),
        ],
        in_specs=[pl.BlockSpec(memory_space=vmem)] * 4,
        out_specs=[pl.BlockSpec(memory_space=vmem)] * 3,
        scratch_shapes=scratch,
        compiler_params=pltpu.CompilerParams(
            collective_id=0, has_side_effects=True, vmem_limit_bytes=60 * 2**20
        ),
        cost_estimate=pl.CostEstimate(flops=flops, bytes_accessed=12 * R * width, transcendentals=4 * H * R),
    )(image_emb, text_emb, *ids)
    return (loss[0], grad_image, grad_text)


def solution(mesh):
    in_specs = (P("dp", "feat"), P("dp", "feat"), P("dp"), P("dp"))
    out_specs = (P("dp"), P("dp", "feat"), P("dp", "feat"))
    body = functools.partial(per_device, mesh.shape["dp"], 4)
    return jax.shard_map(body, mesh=mesh, in_specs=in_specs, out_specs=out_specs, check_vma=False)
```

```python
import functools
import math

import jax
import jax.numpy as jnp
from jax import lax
from jax.experimental import pallas as pl
from jax.experimental.pallas import tpu as pltpu
from jax.sharding import PartitionSpec as P

HOPS = 2
MESH = pl.DeviceIdType.MESH
TEMPER = 3.0
BIAS = -4.0

F32 = jnp.float32
BF16 = jnp.bfloat16
LIFT = 2.0**48


def log1p_of(x):
    return jnp.where(x < 1e-3, x * (1.0 - 0.5 * x), jnp.log(1.0 + x))


def join(a, b):
    return a + b + a * b


def code(x):
    x = x * LIFT
    return (x * jnp.abs(x)).astype(BF16)


def decode(y):
    y = y.astype(F32)
    x = jnp.sqrt(jnp.abs(y)) * (1.0 / LIFT)
    return jnp.where(y < 0, -x, x)


def by_rows(n, step, body):
    def at(i, carry):
        body(pl.multiple_of(i * step, step))
        return carry

    lax.fori_loop(0, n // step, at, 0)


def kernel(
    n_dp, n_parts, scale, img, txt, iid, tid, loss_o, gi_o, gt_o,
    X, ST, IDS, SID, GV, GS, CS, CV, YS, YR, XS, RX, LV, LS, LOS, LOR, LFIN,
    xs, xr, cs, cr, ys, yr, ids_s, ids_r, gs_s, gs_r, rs, rr, cvs, cvr, os, orr, los, lor,
):
    WD, R = img.shape
    H = R // 2
    C = R // n_parts
    NH = n_parts // 2
    KW = 2 * WD
    STEP = 96
    d = lax.axis_index("dp")
    f = lax.axis_index("feat")
    n_cell = n_dp // 2
    c = d // 2
    a = lax.rem(d, 2)
    flip = c // (n_cell // 2)
    role = lax.rem(f + flip, 2)
    other = 1 - f
    c_next = lax.rem(c + 1, n_cell)
    c_last = lax.rem(c + n_cell - 1, n_cell)
    f_next = lax.rem(role + c_next // (n_cell // 2), 2)
    f_last = lax.rem(role + c_last // (n_cell // 2), 2)
    partner = (d, other)
    core = (2 * c + 1 - a, f)
    diag = (2 * c + 1 - a, other)

    def nxt(core_index):
        return (2 * c_next + core_index, f_next)

    def last(core_index):
        return (2 * c_last + core_index, f_last)

    own_at = pl.multiple_of(f * WD, WD)
    oth_at = pl.multiple_of(other * WD, WD)
    own_half, oth_half = pl.ds(own_at, WD), pl.ds(oth_at, WD)
    a_part = pl.ds(pl.multiple_of(a * H, H), H)

    def chunk(j):
        return pl.ds(pl.multiple_of(j * C, C), C) if not isinstance(j, int) else pl.ds(j * C, C)

    def rcopy(src, dst, ssem, rsem, dev):
        return pltpu.make_async_remote_copy(
            src_ref=src, dst_ref=dst, send_sem=ssem, recv_sem=rsem, device_id=dev, device_id_type=MESH
        )

    def got(dst, rsem):
        pltpu.make_async_copy(dst, dst, rsem).wait()

    def sent(src, ssem):
        pltpu.make_async_copy(src, src, ssem).wait()

    barrier = pltpu.get_barrier_semaphore()
    peers = [partner, core, diag, nxt(0), nxt(1), last(0), last(1)]
    for dev in peers:
        pl.semaphore_signal(barrier, inc=1, device_id=dev, device_id_type=MESH)
    pl.semaphore_wait(barrier, len(peers))

    raws = (img, txt)

    def send_raw(kind, slot):
        raw = raws[kind]
        for j in range(n_parts):
            rcopy(raw.at[:, chunk(j)], X.at[slot, own_half, chunk(j)], xs.at[kind, j], xr.at[kind, j], partner).start()

    def raw_sent(kind):
        for j in range(n_parts):
            sent(raws[kind].at[:, chunk(j)], xs.at[kind, j])

    def place(kind, slot):
        def some(i):
            X[slot, pl.ds(pl.multiple_of(own_at + i, STEP), STEP), :] = raws[kind][pl.ds(i, STEP), :]

        by_rows(WD, STEP, some)

    def assemble(kind, slot, j):
        got(X.at[slot, oth_half, chunk(j)], xr.at[kind, j])

    def whole(slot, j):
        return X.at[slot, :, chunk(j)]

    def to_core(slot, j):
        rcopy(whole(slot, j), whole(slot, j), cs.at[slot, j], cr.at[slot, j], core).start()

    def from_core(slot, j):
        got(whole(slot, j), cr.at[slot, j])

    def to_core_sent(slot, j):
        sent(whole(slot, j), cs.at[slot, j])

    def move(slot, j, dev):
        rcopy(whole(slot, j), whole(3, j), ys.at[j], yr.at[j], dev).start()

    def ids_to_core(slot):
        rcopy(IDS.at[slot], IDS.at[slot], ids_s.at[slot], ids_r.at[slot], core).start()

    def ids_move(slot, k, dev):
        rcopy(IDS.at[slot], IDS.at[3], ids_s.at[3 + k], ids_r.at[3], dev).start()

    def ids_of(slot):
        got(IDS.at[slot], ids_r.at[slot])

    def column(s_acc, slot):
        for j in range(n_parts):
            row = IDS[slot, 0:1, chunk(j)]
            SID[s_acc, chunk(j), :] = jnp.transpose(jnp.broadcast_to(row, (128, C)))

    def units(pairs, s_slot, s_acc, j, image_rows):
        right = X[s_slot, :, chunk(j)]
        ST[...] = jnp.transpose(right)
        sid = jnp.concatenate([SID[s_acc, chunk(j), :]] * (H // 128), axis=1)
        s_sum = None
        for v, v_slot in pairs:
            left = X[v_slot, :, a_part]
            scores = jnp.dot(ST[...], left, preferred_element_type=F32)
            logits = scale * scores + BIAS
            same = sid == IDS[v_slot, 0:1, a_part]
            z = jnp.where(same, -logits, logits)
            e = jnp.exp(-jnp.abs(z))
            inv = 1.0 / (1.0 + e)
            sig = jnp.where(z >= 0, inv, e * inv)
            w = jnp.where(same, -sig, sig).astype(BF16)
            total, prod = jnp.maximum(z, 0.0), e
            if image_rows:
                while total.shape[0] > 8:
                    n = total.shape[0] // 2
                    total = total[:n] + total[n:]
                    prod = join(prod[:n], prod[n:])
                LV[v] += total + log1p_of(prod)
            else:
                while total.shape[1] > 128:
                    n = total.shape[1] // 2
                    total = total[:, :n] + total[:, n:]
                    prod = join(prod[:, :n], prod[:, n:])
                LS[0, chunk(j), :] += total
                LS[1, chunk(j), :] = join(LS[1, chunk(j), :], prod)
            GV[v] += jnp.dot(right, w, preferred_element_type=F32)
            part = lax.dot_general(left, w, (((1,), (1,)), ((), ())), preferred_element_type=F32)
            s_sum = part if s_sum is None else s_sum + part
        GS[s_acc, :, chunk(j)] = s_sum

    def rows_at(base, i):
        return pl.ds(pl.multiple_of(base + i, STEP), STEP)

    def give(b, k, value, kind, dst, dev):
        def some(i):
            XS[b, pl.ds(i, STEP), chunk(k)] = code(scale * value(rows_at(oth_at, i)))

        by_rows(WD, STEP, some)
        rcopy(XS.at[b, :, chunk(k)], RX.at[kind, :, chunk(dst)], os.at[b, k], orr.at[kind, dst], dev).start()

    def given(b, k):
        sent(XS.at[b, :, chunk(k)], os.at[b, k])

    def keep(out, j, value):
        def some(i):
            out[pl.ds(i, STEP), chunk(j)] = scale * value(rows_at(own_at, i))

        by_rows(WD, STEP, some)

    def keep_taken(out, kind, plus):
        def one(j, carry):
            got(RX.at[kind, :, chunk(j)], orr.at[kind, j])

            def some(i):
                value = decode(RX[kind, pl.ds(i, STEP), chunk(j)])
                out[pl.ds(i, STEP), chunk(j)] = out[pl.ds(i, STEP), chunk(j)] + value if plus else value

            by_rows(WD, STEP, some)
            return carry

        lax.fori_loop(0, n_parts, one, 0)

    def turn_back(v, dev):
        for k in range(NH):

            def some(i):
                YS[pl.ds(i, STEP), chunk(k)] = code(GV[v, pl.ds(i, STEP), chunk(k)])

            by_rows(KW, STEP, some)
            rcopy(YS.at[:, chunk(k)], YR.at[:, chunk(k)], rs.at[k], rr.at[k], dev).start()

    def turned_back():
        for k in range(NH):
            sent(YS.at[:, chunk(k)], rs.at[k])

    def v_value(v, k, returned):
        if returned:
            return lambda rows: GV[v, rows, chunk(k)] + decode(YR[rows, chunk(k)])
        return lambda rows: GV[v, rows, chunk(k)]

    def returned(k):
        got(YR.at[:, chunk(k)], rr.at[k])

    def cv_send(k, value):
        def some(i):
            CV[0, pl.ds(i, STEP), chunk(k)] = scale * value(rows_at(own_at, i))

        by_rows(WD, STEP, some)
        rcopy(CV.at[0, :, chunk(k)], CV.at[1, :, chunk(k)], cvs.at[k], cvr.at[k], core).start()

    def cv_keep(out, k, j):
        got(CV.at[1, :, chunk(k)], cvr.at[k])

        def some(i):
            out[pl.ds(i, STEP), chunk(j)] = CV[1, pl.ds(i, STEP), chunk(k)]

        by_rows(WD, STEP, some)

    def cv_sent():
        for k in range(NH):
            sent(CV.at[0, :, chunk(k)], cvs.at[k])

    def s_part(s_acc, j):
        rcopy(GS.at[s_acc, :, chunk(j)], CS.at[:, chunk(j)], gs_s.at[j], gs_r.at[j], core).start()

    def s_part_sent(s_acc):
        for j in range(n_parts):
            sent(GS.at[s_acc, :, chunk(j)], gs_s.at[j])

    def s_home(s_acc, j, out, b, kind, dev):
        got(CS.at[:, chunk(j)], gs_r.at[j])

        def value(rows):
            return GS[s_acc, rows, chunk(j)] + CS[rows, chunk(j)]

        give(b, j, value, kind, j, dev)
        keep(out, j, value)

    def zero():
        def some(i):
            for v in range(3):
                GV[v, pl.ds(i, STEP), :] = jnp.zeros((STEP, H), F32)

        by_rows(KW, STEP, some)
        LV[...] = jnp.zeros_like(LV)

    def zero_rows():
        def some(i):
            LS[:, pl.ds(i, C), :] = jnp.zeros((2, C, 128), F32)

        by_rows(R, C, some)

    def row_of(v):
        return jnp.broadcast_to(jnp.sum(LV[v], axis=0, keepdims=True), (8, H))

    def row_of_s(start):
        col = LS[0, start : start + H, :] + log1p_of(LS[1, start : start + H, :])
        row = jnp.sum(jnp.transpose(col), axis=0, keepdims=True)
        return jnp.broadcast_to(row, (8, H))

    mean = 1.0 / float((HOPS + 1) * R)

    def loss_out():
        loss_o[...] = LFIN[0:1, :] * mean

    def loss_to_partner():
        rcopy(LFIN, LFIN, los.at[3], lor.at[3], partner).start()

    def role_0():
        @pl.when(a == 0)
        def _():
            send_raw(1, 1)
            IDS[0] = jnp.broadcast_to(iid[...], (8, R))
            IDS[1] = jnp.broadcast_to(tid[...], (8, R))
            ids_to_core(0)
            ids_to_core(1)
            ids_move(0, 0, last(0))
            ids_move(0, 1, last(1))
            place(0, 0)
            place(1, 1)

        @pl.when(a == 1)
        def _():
            send_raw(1, 2)
            send_raw(0, 0)
            IDS[2] = jnp.broadcast_to(tid[...], (8, R))
            ids_to_core(2)
            place(1, 2)

        zero()

        @pl.when(a == 0)
        def _():
            ids_of(2)
            ids_of(3)
            column(0, 2)
            column(1, 1)
            for j in range(n_parts):
                assemble(0, 0, j)
                if j >= NH:
                    to_core(0, j)
                move(0, j, last(j // NH))

        @pl.when(a == 1)
        def _():
            ids_of(0)
            ids_of(1)
            ids_of(3)
            column(0, 2)
            column(1, 1)
            for j in range(n_parts):
                assemble(1, 2, j)
                to_core(2, j)

        for k in range(NH):
            got(whole(3, a * NH + k), yr.at[a * NH + k])

        def first(j, carry):
            pl.when(a == 0)(lambda: from_core(2, j))
            units([(1, 3)], 2, 0, j, True)
            pl.when(a == 0)(lambda: s_part(0, j))

            @pl.when((a == 1) & (j > 0))
            def _():
                s_home(0, j - 1, gt_o, 1, 1, partner)

            return carry

        lax.fori_loop(0, n_parts, first, 0)

        @pl.when(a == 1)
        def _():
            s_home(0, n_parts - 1, gt_o, 1, 1, partner)
            for j in range(NH, n_parts):
                from_core(0, j)

        def second(j, carry):
            @pl.when(a == 0)
            def _():
                assemble(1, 1, j)
                to_core(1, j)

            pl.when(a == 1)(lambda: from_core(1, j))
            units([(0, 0), (1, 3)], 1, 1, j, True)
            pl.when(a == 1)(lambda: s_part(1, j))

            @pl.when((a == 0) & (j > 0))
            def _():
                s_home(1, j - 1, gt_o, 1, 1, partner)

            return carry

        lax.fori_loop(0, n_parts, second, 0)
        turn_back(1, nxt(a))

        LOS[0] = row_of(0)
        LOS[1] = row_of(1)
        rcopy(LOS.at[1], LOR.at[1 + a], los.at[1], lor.at[1 + a], nxt(0)).start()

        @pl.when(a == 1)
        def _():
            rcopy(LOS.at[0], LOR.at[0], los.at[0], lor.at[0], core).start()

        @pl.when(a == 0)
        def _():
            s_home(1, n_parts - 1, gt_o, 1, 1, partner)
            for i in range(3):
                got(LOR.at[i], lor.at[i])
            LFIN[:, 0:H] = LOS[0] + LOR[1]
            LFIN[:, H:R] = LOR[0] + LOR[2]
            loss_to_partner()
            loss_out()
            for k in range(NH):
                returned(k)
                give(0, k, v_value(0, k, True), 0, k, partner)
                keep(gi_o, k, v_value(0, k, True))
            keep_taken(gt_o, 1, True)
            for k in range(NH):
                cv_keep(gi_o, k, NH + k)
            raw_sent(1)
            for j in range(n_parts):
                to_core_sent(1, j)
                sent(whole(0, j), ys.at[j])
            for j in range(NH, n_parts):
                to_core_sent(0, j)
            for k in (0, 1, 3, 4):
                sent(IDS.at[0], ids_s.at[k])
            s_part_sent(0)
            sent(LFIN, los.at[3])

        @pl.when(a == 1)
        def _():
            for k in range(NH):
                returned(k)
                give(0, k, v_value(0, k, True), 0, NH + k, diag)
                cv_send(k, v_value(0, k, True))
            keep_taken(gt_o, 1, True)
            keep_taken(gi_o, 0, False)
            got(LFIN, lor.at[3])
            loss_out()
            raw_sent(0)
            raw_sent(1)
            for j in range(n_parts):
                to_core_sent(2, j)
            sent(IDS.at[2], ids_s.at[2])
            s_part_sent(1)
            sent(LOS.at[0], los.at[0])
            cv_sent()

        for k in range(NH):
            given(0, k)
        for j in range(n_parts):
            given(1, j)
        sent(LOS.at[1], los.at[1])
        turned_back()

    def role_1():
        @pl.when(a == 0)
        def _():
            send_raw(0, 0)
            send_raw(1, 1)
            IDS[1] = jnp.broadcast_to(tid[...], (8, R))
            ids_to_core(1)
            place(1, 1)

        @pl.when(a == 1)
        def _():
            send_raw(1, 2)
            IDS[0] = jnp.broadcast_to(iid[...], (8, R))
            IDS[2] = jnp.broadcast_to(tid[...], (8, R))
            ids_to_core(0)
            ids_to_core(2)
            ids_move(2, 0, nxt(0))
            ids_move(2, 1, nxt(1))
            place(1, 2)
            place(0, 0)

        zero()
        zero_rows()

        @pl.when(a == 0)
        def _():
            ids_of(0)
            ids_of(2)
            ids_of(3)
            column(0, 0)
            for j in range(n_parts):
                assemble(1, 1, j)
                if j >= NH:
                    to_core(1, j)
            for j in range(NH):
                from_core(2, j)

        @pl.when(a == 1)
        def _():
            ids_of(1)
            ids_of(3)
            column(0, 0)
            for j in range(n_parts):
                assemble(1, 2, j)
                if j < NH:
                    to_core(2, j)
                move(2, j, nxt(j // NH))
            for j in range(NH, n_parts):
                from_core(1, j)

        for k in range(NH):
            got(whole(3, a * NH + k), yr.at[a * NH + k])

        def step(j, carry):
            @pl.when(a == 1)
            def _():
                assemble(0, 0, j)
                to_core(0, j)

            pl.when(a == 0)(lambda: from_core(0, j))
            units([(1, 1), (0, 2), (2, 3)], 0, 0, j, False)
            pl.when(a == 0)(lambda: s_part(0, j))

            @pl.when((a == 1) & (j > 0))
            def _():
                s_home(0, j - 1, gi_o, 2, 0, partner)

            return carry

        lax.fori_loop(0, n_parts, step, 0)
        turn_back(2, last(a))

        @pl.when(a == 0)
        def _():
            LOS[0] = row_of_s(0)
            LOS[1] = row_of_s(H)
            for i in range(2):
                rcopy(LOS.at[i], LOR.at[i], los.at[i], lor.at[i], core).start()
            for k in range(NH):
                give(1, k, v_value(1, k, False), 1, k, partner)
                keep(gt_o, k, v_value(1, k, False))
            for k in range(NH):
                returned(k)
                give(0, k, v_value(0, k, True), 1, k, diag)
                cv_send(k, v_value(0, k, True))
            for k in range(NH):
                cv_keep(gt_o, k, NH + k)
            keep_taken(gt_o, 1, True)
            keep_taken(gi_o, 0, False)
            got(LFIN, lor.at[3])
            loss_out()
            raw_sent(0)
            raw_sent(1)
            for j in range(NH, n_parts):
                to_core_sent(1, j)
            sent(IDS.at[1], ids_s.at[1])
            s_part_sent(0)
            for i in range(2):
                sent(LOS.at[i], los.at[i])

        @pl.when(a == 1)
        def _():
            s_home(0, n_parts - 1, gi_o, 2, 0, partner)
            for k in range(NH):
                give(1, k, v_value(1, k, False), 1, NH + k, diag)
                cv_send(k, v_value(1, k, False))
            for i in range(2):
                got(LOR.at[i], lor.at[i])
                LFIN[:, i * H : (i + 1) * H] = row_of_s(i * H) + LOR[i]
            loss_to_partner()
            loss_out()
            for k in range(NH):
                returned(k)
                give(0, k, v_value(0, k, True), 1, NH + k, partner)
                keep(gt_o, NH + k, v_value(0, k, True))
            for k in range(NH):
                cv_keep(gt_o, k, k)
            keep_taken(gt_o, 1, True)
            raw_sent(1)
            for j in range(n_parts):
                to_core_sent(0, j)
                sent(whole(2, j), ys.at[j])
            for j in range(NH):
                to_core_sent(2, j)
            for k in (0, 2, 3, 4):
                sent(IDS.at[0], ids_s.at[k])
            for j in range(n_parts):
                given(2, j)
            sent(LFIN, los.at[3])

        for k in range(NH):
            given(0, k)
            given(1, k)
        turned_back()
        cv_sent()

    pl.when(role == 0)(role_0)
    pl.when(role == 1)(role_1)


def per_device(n_dp, n_parts, image_emb, text_emb, image_ids, text_ids):
    R, width = image_emb.shape
    H, C = R // 2, R // n_parts
    KW = 2 * width
    scale = TEMPER / math.sqrt(KW)
    ids = [i[None, :] for i in (image_ids, text_ids)]
    dma = pltpu.SemaphoreType.DMA
    vmem = pltpu.VMEM
    scratch = [
        vmem((4, KW, R), BF16),
        vmem((C, KW), BF16),
        vmem((4, 8, R), jnp.int32),
        vmem((2, R, 128), jnp.int32),
        vmem((3, KW, H), F32),
        vmem((2, KW, R), F32),
        vmem((KW, R), F32),
        vmem((2, width, H), F32),
        vmem((KW, H), BF16),
        vmem((KW, H), BF16),
        vmem((3, width, R), BF16),
        vmem((2, width, R), BF16),
        vmem((2, 8, H), F32),
        vmem((2, R, 128), F32),
        vmem((2, 8, H), F32),
        vmem((3, 8, H), F32),
        vmem((8, R), F32),
        dma((2, n_parts)), dma((2, n_parts)),
        dma((3, n_parts)), dma((3, n_parts)),
        dma((n_parts,)), dma((n_parts,)),
        dma((5,)), dma((4,)),
        dma((n_parts,)), dma((n_parts,)),
        dma((n_parts,)), dma((n_parts,)),
        dma((n_parts,)), dma((n_parts,)),
        dma((3, n_parts)), dma((2, n_parts)),
        dma((4,)), dma((4,)),
    ]
    flops = 9 * 2 * H * R * KW
    loss, grad_image, grad_text = pl.pallas_call(
        functools.partial(kernel, n_dp, n_parts, scale),
        out_shape=[
            jax.ShapeDtypeStruct((1, R), F32),
            jax.ShapeDtypeStruct((width, R), F32),
            jax.ShapeDtypeStruct((width, R), F32),
        ],
        in_specs=[pl.BlockSpec(memory_space=vmem)] * 4,
        out_specs=[pl.BlockSpec(memory_space=vmem)] * 3,
        scratch_shapes=scratch,
        compiler_params=pltpu.CompilerParams(
            collective_id=0, has_side_effects=True, vmem_limit_bytes=60 * 2**20
        ),
        cost_estimate=pl.CostEstimate(flops=flops, bytes_accessed=12 * R * width, transcendentals=4 * H * R),
    )(image_emb.T, text_emb.T, *ids)
    return (loss[0], grad_image.T, grad_text.T)


def solution(mesh):
    in_specs = (P("dp", "feat"), P("dp", "feat"), P("dp"), P("dp"))
    out_specs = (P("dp"), P("dp", "feat"), P("dp", "feat"))
    body = functools.partial(per_device, mesh.shape["dp"], 4)
    return jax.shard_map(body, mesh=mesh, in_specs=in_specs, out_specs=out_specs, check_vma=False)
```

```python
import functools
import math

import jax
import jax.numpy as jnp
from jax import lax
from jax.experimental import pallas as pl
from jax.experimental.pallas import tpu as pltpu
from jax.sharding import PartitionSpec as P

HOPS = 2
MESH = pl.DeviceIdType.MESH
TEMPER = 3.0
BIAS = -4.0

F32 = jnp.float32
BF16 = jnp.bfloat16
LIFT = 2.0**48
LOG2E = 1.4426950408889634
LN2 = 0.6931471805599453


def log1p_of(x):
    return jnp.where(x < 1e-3, x * (1.0 - 0.5 * x), jnp.log(1.0 + x))


def join(a, b):
    return a + b + a * b


def code(x):
    x = x * LIFT
    return (x * jnp.abs(x)).astype(BF16)


def decode(y):
    y = y.astype(F32)
    x = jnp.sqrt(jnp.abs(y)) * (1.0 / LIFT)
    return jnp.where(y < 0, -x, x)


def by_rows(n, step, body):
    def at(i, carry):
        body(pl.multiple_of(i * step, step))
        return carry

    lax.fori_loop(0, n // step, at, 0)


def kernel(
    n_dp, n_parts, scale, img, txt, iid, tid, loss_o, gi_o, gt_o,
    X, ST, IDS, SID, GV, GS, CS, CV, YS, YR, XS, RX, LV, LS, LOS, LOR, LFIN,
    xs, xr, cs, cr, ys, yr, ids_s, ids_r, gs_s, gs_r, rs, rr, cvs, cvr, os, orr, los, lor,
):
    WD, R = img.shape
    H = R // 2
    C = R // n_parts
    NH = n_parts // 2
    N_PIECES = R // 128
    PER = C // 128
    KW = 2 * WD
    STEP = 96
    d = lax.axis_index("dp")
    f = lax.axis_index("feat")
    n_cell = n_dp // 2
    c = d // 2
    a = lax.rem(d, 2)
    flip = c // (n_cell // 2)
    role = lax.rem(f + flip, 2)
    other = 1 - f
    c_next = lax.rem(c + 1, n_cell)
    c_last = lax.rem(c + n_cell - 1, n_cell)
    f_next = lax.rem(role + c_next // (n_cell // 2), 2)
    f_last = lax.rem(role + c_last // (n_cell // 2), 2)
    partner = (d, other)
    core = (2 * c + 1 - a, f)
    diag = (2 * c + 1 - a, other)

    def nxt(core_index):
        return (2 * c_next + core_index, f_next)

    def last(core_index):
        return (2 * c_last + core_index, f_last)

    own_at = pl.multiple_of(f * WD, WD)
    oth_at = pl.multiple_of(other * WD, WD)
    own_half, oth_half = pl.ds(own_at, WD), pl.ds(oth_at, WD)
    a_part = pl.ds(pl.multiple_of(a * H, H), H)

    def chunk(j):
        return pl.ds(pl.multiple_of(j * C, C), C) if not isinstance(j, int) else pl.ds(j * C, C)

    def piece(q):
        return pl.ds(pl.multiple_of(q * 128, 128), 128) if not isinstance(q, int) else pl.ds(q * 128, 128)

    def rcopy(src, dst, ssem, rsem, dev):
        return pltpu.make_async_remote_copy(
            src_ref=src, dst_ref=dst, send_sem=ssem, recv_sem=rsem, device_id=dev, device_id_type=MESH
        )

    def got(dst, rsem):
        pltpu.make_async_copy(dst, dst, rsem).wait()

    def sent(src, ssem):
        pltpu.make_async_copy(src, src, ssem).wait()

    barrier = pltpu.get_barrier_semaphore()
    near = (partner, core, diag)

    def arrive(far, senders):
        for dev in (*near, far):
            pl.semaphore_signal(barrier, inc=1, device_id=dev, device_id_type=MESH)
        pl.when(a == senders)(lambda: pl.semaphore_wait(barrier, len(near) + 2))
        pl.when(a != senders)(lambda: pl.semaphore_wait(barrier, len(near)))

    raws = (img, txt)

    def send_raw(kind, slot):
        raw = raws[kind]
        for j in range(n_parts):
            rcopy(raw.at[:, chunk(j)], X.at[slot, own_half, chunk(j)], xs.at[kind, j], xr.at[kind, j], partner).start()

    def raw_sent(kind):
        for j in range(n_parts):
            sent(raws[kind].at[:, chunk(j)], xs.at[kind, j])

    def place(kind, slot):
        def some(i):
            X[slot, pl.ds(pl.multiple_of(own_at + i, STEP), STEP), :] = raws[kind][pl.ds(i, STEP), :]

        by_rows(WD, STEP, some)

    def assemble(kind, slot, j):
        got(X.at[slot, oth_half, chunk(j)], xr.at[kind, j])

    def whole(slot, j):
        return X.at[slot, :, chunk(j)]

    def to_core(slot, j):
        rcopy(whole(slot, j), whole(slot, j), cs.at[slot, j], cr.at[slot, j], core).start()

    def from_core(slot, j):
        got(whole(slot, j), cr.at[slot, j])

    def to_core_sent(slot, j):
        sent(whole(slot, j), cs.at[slot, j])

    def move(slot, j, dev):
        rcopy(whole(slot, j), whole(3, j), ys.at[j], yr.at[j], dev).start()

    def ids_to_core(slot):
        rcopy(IDS.at[slot], IDS.at[slot], ids_s.at[slot], ids_r.at[slot], core).start()

    def ids_move(slot, k, dev):
        rcopy(IDS.at[slot], IDS.at[3], ids_s.at[3 + k], ids_r.at[3], dev).start()

    def ids_of(slot):
        got(IDS.at[slot], ids_r.at[slot])

    def column(s_acc, slot):
        for j in range(n_parts):
            row = IDS[slot, 0:1, chunk(j)]
            SID[s_acc, chunk(j), :] = jnp.transpose(jnp.broadcast_to(row, (128, C)))

    def units(pairs, s_slot, s_acc, j, image_rows, first=True):
        right = X[s_slot, :, chunk(j)]
        if first:
            ST[s_acc, chunk(j), :] = jnp.transpose(right)
        sid = jnp.concatenate([SID[s_acc, chunk(j), :]] * (H // 128), axis=1)
        s_sum = None
        lefts = [X[v_slot, :, a_part] for _, v_slot in pairs]
        scores = [jnp.dot(ST[s_acc, chunk(j), :], left, preferred_element_type=F32) for left in lefts]
        for (v, v_slot), left, score in zip(pairs, lefts, scores):
            logits = (scale * LOG2E) * score + BIAS * LOG2E
            same = sid == IDS[v_slot, 0:1, a_part]
            e = jnp.exp2(-jnp.abs(logits))
            den = 1.0 + e
            inv = pl.reciprocal(den, approx=True)
            inv = inv * (2.0 - den * inv)
            z = jnp.where(same, -logits, logits)
            sig = jnp.where(z >= 0, inv, e * inv)
            w = jnp.where(same, -sig, sig).astype(BF16)
            total, prod = jnp.maximum(z, 0.0), e
            if image_rows:
                while total.shape[0] > 8:
                    n = total.shape[0] // 2
                    total = total[:n] + total[n:]
                    prod = join(prod[:n], prod[n:])
                LV[v] += LN2 * total + log1p_of(prod)
            else:
                while total.shape[1] > 128:
                    n = total.shape[1] // 2
                    total = total[:, :n] + total[:, n:]
                    prod = join(prod[:, :n], prod[:, n:])
                LS[0, chunk(j), :] += total
                LS[1, chunk(j), :] = join(LS[1, chunk(j), :], prod)
            GV[v] += jnp.dot(right, w, preferred_element_type=F32)
            part = lax.dot_general(left, w, (((1,), (1,)), ((), ())), preferred_element_type=F32)
            s_sum = part if s_sum is None else s_sum + part
        if first:
            GS[s_acc, :, chunk(j)] = s_sum
        else:
            GS[s_acc, :, chunk(j)] += s_sum

    def rows_at(base, i):
        return pl.ds(pl.multiple_of(base + i, STEP), STEP)

    def give(b, q, value, kind, dst, dev):
        def some(i):
            XS[b, pl.ds(i, STEP), piece(q)] = code(scale * value(rows_at(oth_at, i)))

        by_rows(WD, STEP, some)
        rcopy(XS.at[b, :, piece(q)], RX.at[kind, :, piece(dst)], os.at[b, q], orr.at[kind, dst], dev).start()

    def given(b, n):
        def one(q, carry):
            sent(XS.at[b, :, piece(q)], os.at[b, q])
            return carry

        lax.fori_loop(0, n, one, 0)

    def keep(out, q, value, plus=False):
        def some(i):
            mine = scale * value(rows_at(own_at, i))
            out[pl.ds(i, STEP), piece(q)] = out[pl.ds(i, STEP), piece(q)] + mine if plus else mine

        by_rows(WD, STEP, some)

    def taken(out, kind, q, plus):
        got(RX.at[kind, :, piece(q)], orr.at[kind, q])

        def some(i):
            value = decode(RX[kind, pl.ds(i, STEP), piece(q)])
            out[pl.ds(i, STEP), piece(q)] = out[pl.ds(i, STEP), piece(q)] + value if plus else value

        by_rows(WD, STEP, some)

    def taken_from_both(out, kind, plus):
        def one(q):
            taken(out, kind, q, plus)
            taken(out, kind, N_PIECES // 2 + q, plus)

        over(N_PIECES // 2, one)

    def over(n, body):
        def one(q, carry):
            body(q)
            return carry

        lax.fori_loop(0, n, one, 0)

    def turn_back(v, dev):
        def one(q):
            def some(i):
                YS[pl.ds(i, STEP), piece(q)] = code(GV[v, pl.ds(i, STEP), piece(q)])

            by_rows(KW, STEP, some)
            rcopy(YS.at[:, piece(q)], YR.at[:, piece(q)], rs.at[q], rr.at[q], dev).start()

        over(N_PIECES // 2, one)

    def turned_back():
        over(N_PIECES // 2, lambda q: sent(YS.at[:, piece(q)], rs.at[q]))

    def v_value(v, q):
        return lambda rows: GV[v, rows, piece(q)]

    def with_returned(v, q):
        got(YR.at[:, piece(q)], rr.at[q])
        return lambda rows: GV[v, rows, piece(q)] + decode(YR[rows, piece(q)])

    def cv_send(q, value):
        def some(i):
            CV[0, pl.ds(i, STEP), piece(q)] = scale * value(rows_at(own_at, i))

        by_rows(WD, STEP, some)
        rcopy(CV.at[0, :, piece(q)], CV.at[1, :, piece(q)], cvs.at[q], cvr.at[q], core).start()

    def cv_keep(out, base, plus=False):
        def one(q):
            got(CV.at[1, :, piece(q)], cvr.at[q])

            def some(i):
                mine = CV[1, pl.ds(i, STEP), piece(q)]
                at = (pl.ds(i, STEP), piece(base + q))
                out[at] = out[at] + mine if plus else mine

            by_rows(WD, STEP, some)

        over(N_PIECES // 2, one)

    def cv_sent():
        over(N_PIECES // 2, lambda q: sent(CV.at[0, :, piece(q)], cvs.at[q]))

    def s_part(s_acc, j):
        rcopy(GS.at[s_acc, :, chunk(j)], CS.at[:, chunk(j)], gs_s.at[j], gs_r.at[j], core).start()

    def s_part_sent(s_acc):
        for j in range(n_parts):
            sent(GS.at[s_acc, :, chunk(j)], gs_s.at[j])

    def s_home(s_acc, j, out, b, kind, dev):
        got(CS.at[:, chunk(j)], gs_r.at[j])

        def one(i):
            q = j * PER + i

            def value(rows):
                return GS[s_acc, rows, piece(q)] + CS[rows, piece(q)]

            give(b, q, value, kind, q, dev)
            keep(out, q, value)

        over(PER, one)

    def zero():
        def some(i):
            for v in range(3):
                GV[v, pl.ds(i, STEP), :] = jnp.zeros((STEP, H), F32)

        by_rows(KW, STEP, some)
        LV[...] = jnp.zeros_like(LV)

    def zero_rows():
        def some(i):
            LS[:, pl.ds(i, C), :] = jnp.zeros((2, C, 128), F32)

        by_rows(R, C, some)

    def row_of(v):
        return jnp.broadcast_to(jnp.sum(LV[v], axis=0, keepdims=True), (8, H))

    def row_of_s(start):
        col = LN2 * LS[0, start : start + H, :] + log1p_of(LS[1, start : start + H, :])
        row = jnp.sum(jnp.transpose(col), axis=0, keepdims=True)
        return jnp.broadcast_to(row, (8, H))

    mean = 1.0 / float((HOPS + 1) * R)

    def loss_out():
        loss_o[...] = LFIN[0:1, :] * mean

    def loss_to_partner():
        rcopy(LFIN, LFIN, los.at[3], lor.at[3], partner).start()

    def role_0():
        arrive(nxt(0), 0)

        @pl.when(a == 0)
        def _():
            send_raw(1, 1)
            IDS[0] = jnp.broadcast_to(iid[...], (8, R))
            IDS[1] = jnp.broadcast_to(tid[...], (8, R))
            ids_to_core(0)
            ids_to_core(1)
            ids_move(0, 0, last(0))
            ids_move(0, 1, last(1))
            place(0, 0)
            place(1, 1)

        @pl.when(a == 1)
        def _():
            send_raw(1, 2)
            send_raw(0, 0)
            IDS[2] = jnp.broadcast_to(tid[...], (8, R))
            ids_to_core(2)
            place(1, 2)

        zero()

        @pl.when(a == 0)
        def _():
            ids_of(2)
            ids_of(3)
            column(0, 2)
            column(1, 1)
            for j in range(n_parts):
                assemble(0, 0, j)
                if j >= NH:
                    to_core(0, j)
                move(0, j, last(j // NH))

        @pl.when(a == 1)
        def _():
            ids_of(0)
            ids_of(1)
            ids_of(3)
            column(0, 2)
            column(1, 1)
            for j in range(n_parts):
                assemble(1, 2, j)
                to_core(2, j)

        for k in range(NH):
            got(whole(3, a * NH + k), yr.at[a * NH + k])

        def first(j, carry):
            pl.when(a == 0)(lambda: from_core(2, j))
            units([(1, 3)], 2, 0, j, True)
            pl.when(a == 0)(lambda: s_part(0, j))

            @pl.when((a == 1) & (j > 0))
            def _():
                s_home(0, j - 1, gt_o, 1, 1, partner)

            return carry

        lax.fori_loop(0, n_parts, first, 0)

        @pl.when(a == 1)
        def _():
            s_home(0, n_parts - 1, gt_o, 1, 1, partner)

        def second(j, carry):
            @pl.when(a == 0)
            def _():
                assemble(1, 1, j)
                to_core(1, j)

            pl.when(a == 1)(lambda: from_core(1, j))
            units([(1, 3)], 1, 1, j, True)
            return carry

        lax.fori_loop(0, n_parts, second, 0)
        turn_back(1, nxt(a))

        @pl.when(a == 1)
        def _():
            for j in range(NH, n_parts):
                from_core(0, j)

        def third(j, carry):
            units([(0, 0)], 1, 1, j, True, first=False)
            pl.when(a == 1)(lambda: s_part(1, j))

            @pl.when((a == 0) & (j > 0))
            def _():
                s_home(1, j - 1, gt_o, 1, 1, partner)

            return carry

        lax.fori_loop(0, n_parts, third, 0)
        LOS[0] = row_of(0)
        LOS[1] = row_of(1)
        rcopy(LOS.at[1], LOR.at[1 + a], los.at[1], lor.at[1 + a], nxt(0)).start()

        @pl.when(a == 1)
        def _():
            rcopy(LOS.at[0], LOR.at[0], los.at[0], lor.at[0], core).start()

        @pl.when(a == 0)
        def _():
            s_home(1, n_parts - 1, gt_o, 1, 1, partner)
            for i in range(3):
                got(LOR.at[i], lor.at[i])
            LFIN[:, 0:H] = LOS[0] + LOR[1]
            LFIN[:, H:R] = LOR[0] + LOR[2]
            loss_to_partner()
            loss_out()

            def one(q):
                value = with_returned(0, q)
                give(0, q, value, 0, q, partner)
                keep(gi_o, q, value)
                taken(gt_o, 1, q, True)
                taken(gt_o, 1, N_PIECES // 2 + q, True)

            over(N_PIECES // 2, one)
            cv_keep(gi_o, N_PIECES // 2)
            raw_sent(1)
            for j in range(n_parts):
                to_core_sent(1, j)
                sent(whole(0, j), ys.at[j])
            for j in range(NH, n_parts):
                to_core_sent(0, j)
            for k in (0, 1, 3, 4):
                sent(IDS.at[0], ids_s.at[k])
            s_part_sent(0)
            sent(LFIN, los.at[3])

        @pl.when(a == 1)
        def _():
            def one(q):
                value = with_returned(0, q)
                give(0, q, value, 0, N_PIECES // 2 + q, diag)
                cv_send(q, value)
                taken(gi_o, 0, 2 * q, False)
                taken(gi_o, 0, 2 * q + 1, False)

            over(N_PIECES // 2, one)
            got(LFIN, lor.at[3])
            loss_out()
            taken_from_both(gt_o, 1, True)
            raw_sent(0)
            raw_sent(1)
            for j in range(n_parts):
                to_core_sent(2, j)
            sent(IDS.at[2], ids_s.at[2])
            s_part_sent(1)
            sent(LOS.at[0], los.at[0])
            cv_sent()

        given(0, N_PIECES // 2)
        given(1, N_PIECES)
        sent(LOS.at[1], los.at[1])
        turned_back()

    def role_1():
        arrive(last(1), 1)

        @pl.when(a == 0)
        def _():
            send_raw(0, 0)
            send_raw(1, 1)
            IDS[1] = jnp.broadcast_to(tid[...], (8, R))
            ids_to_core(1)
            place(1, 1)

        @pl.when(a == 1)
        def _():
            send_raw(1, 2)
            IDS[0] = jnp.broadcast_to(iid[...], (8, R))
            IDS[2] = jnp.broadcast_to(tid[...], (8, R))
            ids_to_core(0)
            ids_to_core(2)
            ids_move(2, 0, nxt(0))
            ids_move(2, 1, nxt(1))
            place(1, 2)
            place(0, 0)

        zero()
        zero_rows()

        @pl.when(a == 0)
        def _():
            ids_of(0)
            ids_of(2)
            ids_of(3)
            column(0, 0)
            for j in range(n_parts):
                assemble(1, 1, j)
                if j >= NH:
                    to_core(1, j)
            for j in range(NH):
                from_core(2, j)

        @pl.when(a == 1)
        def _():
            ids_of(1)
            ids_of(3)
            column(0, 0)
            for j in range(n_parts):
                assemble(1, 2, j)
                if j < NH:
                    to_core(2, j)
                move(2, j, nxt(j // NH))
            for j in range(NH, n_parts):
                from_core(1, j)

        for k in range(NH):
            got(whole(3, a * NH + k), yr.at[a * NH + k])

        def step(j, carry):
            @pl.when(a == 1)
            def _():
                assemble(0, 0, j)
                to_core(0, j)

            pl.when(a == 0)(lambda: from_core(0, j))
            units([(1, 1), (2, 3)], 0, 0, j, False)
            return carry

        lax.fori_loop(0, n_parts, step, 0)
        turn_back(2, last(a))

        @pl.when(a == 0)
        def _():
            def own(q):
                give(1, q, v_value(1, q), 1, q, partner)
                keep(gt_o, q, v_value(1, q))

            over(N_PIECES // 2, own)

        @pl.when(a == 1)
        def _():
            def own(q):
                give(1, q, v_value(1, q), 1, N_PIECES // 2 + q, diag)
                cv_send(q, v_value(1, q))

            over(N_PIECES // 2, own)

        def final(j, carry):
            units([(0, 2)], 0, 0, j, False, first=False)
            pl.when(a == 0)(lambda: s_part(0, j))

            @pl.when((a == 1) & (j > 0))
            def _():
                s_home(0, j - 1, gi_o, 2, 0, partner)

            return carry

        lax.fori_loop(0, n_parts, final, 0)

        @pl.when(a == 0)
        def _():
            LOS[0] = row_of_s(0)
            LOS[1] = row_of_s(H)
            for i in range(2):
                rcopy(LOS.at[i], LOR.at[i], los.at[i], lor.at[i], core).start()

            def one(q):
                value = with_returned(0, q)
                give(0, q, value, 1, q, diag)
                cv_send(q, value)
                taken(gt_o, 1, 2 * q, True)
                taken(gt_o, 1, 2 * q + 1, True)

            cv_keep(gt_o, N_PIECES // 2)
            over(N_PIECES // 2, one)
            got(LFIN, lor.at[3])
            loss_out()
            taken_from_both(gi_o, 0, False)
            raw_sent(0)
            raw_sent(1)
            for j in range(NH, n_parts):
                to_core_sent(1, j)
            sent(IDS.at[1], ids_s.at[1])
            s_part_sent(0)
            for i in range(2):
                sent(LOS.at[i], los.at[i])

        @pl.when(a == 1)
        def _():
            s_home(0, n_parts - 1, gi_o, 2, 0, partner)
            for i in range(2):
                got(LOR.at[i], lor.at[i])
                LFIN[:, i * H : (i + 1) * H] = row_of_s(i * H) + LOR[i]
            loss_to_partner()
            loss_out()

            def one(q):
                value = with_returned(0, q)
                give(0, q, value, 1, N_PIECES // 2 + q, partner)
                keep(gt_o, N_PIECES // 2 + q, value, plus=True)

            over(N_PIECES, lambda q: taken(gt_o, 1, q, False))
            over(N_PIECES // 2, one)
            cv_keep(gt_o, 0, plus=True)
            raw_sent(1)
            for j in range(n_parts):
                to_core_sent(0, j)
                sent(whole(2, j), ys.at[j])
            for j in range(NH):
                to_core_sent(2, j)
            for k in (0, 2, 3, 4):
                sent(IDS.at[0], ids_s.at[k])
            given(2, N_PIECES)
            sent(LFIN, los.at[3])

        given(0, N_PIECES // 2)
        given(1, N_PIECES // 2)
        turned_back()
        cv_sent()

    pl.when(role == 0)(role_0)
    pl.when(role == 1)(role_1)


def per_device(n_dp, n_parts, image_emb, text_emb, image_ids, text_ids):
    R, width = image_emb.shape
    H, C = R // 2, R // n_parts
    KW = 2 * width
    scale = TEMPER / math.sqrt(KW)
    ids = [i[None, :] for i in (image_ids, text_ids)]
    dma = pltpu.SemaphoreType.DMA
    vmem = pltpu.VMEM
    scratch = [
        vmem((4, KW, R), BF16),
        vmem((2, R, KW), BF16),
        vmem((4, 8, R), jnp.int32),
        vmem((2, R, 128), jnp.int32),
        vmem((3, KW, H), F32),
        vmem((2, KW, R), F32),
        vmem((KW, R), F32),
        vmem((2, width, H), F32),
        vmem((KW, H), BF16),
        vmem((KW, H), BF16),
        vmem((3, width, R), BF16),
        vmem((2, width, R), BF16),
        vmem((2, 8, H), F32),
        vmem((2, R, 128), F32),
        vmem((2, 8, H), F32),
        vmem((3, 8, H), F32),
        vmem((8, R), F32),
        dma((2, n_parts)), dma((2, n_parts)),
        dma((3, n_parts)), dma((3, n_parts)),
        dma((n_parts,)), dma((n_parts,)),
        dma((5,)), dma((4,)),
        dma((n_parts,)), dma((n_parts,)),
        dma((R // 256,)), dma((R // 256,)),
        dma((R // 256,)), dma((R // 256,)),
        dma((3, R // 128)), dma((2, R // 128)),
        dma((4,)), dma((4,)),
    ]
    flops = 9 * 2 * H * R * KW
    loss, grad_image, grad_text = pl.pallas_call(
        functools.partial(kernel, n_dp, n_parts, scale),
        out_shape=[
            pltpu.VMEM((1, R), F32),
            pltpu.VMEM((width, R), F32),
            pltpu.VMEM((width, R), F32),
        ],
        in_specs=[pl.BlockSpec(memory_space=vmem)] * 4,
        out_specs=[pl.BlockSpec(memory_space=vmem)] * 3,
        scratch_shapes=scratch,
        compiler_params=pltpu.CompilerParams(
            collective_id=0, has_side_effects=True, vmem_limit_bytes=54 * 2**20
        ),
        cost_estimate=pl.CostEstimate(flops=flops, bytes_accessed=12 * R * width, transcendentals=4 * H * R),
    )(image_emb.T, text_emb.T, *ids)
    return (loss[0], grad_image.T, grad_text.T)


def solution(mesh):
    in_specs = (P("dp", "feat"), P("dp", "feat"), P("dp"), P("dp"))
    out_specs = (P("dp"), P("dp", "feat"), P("dp", "feat"))
    body = functools.partial(per_device, mesh.shape["dp"], 4)
    return jax.shard_map(body, mesh=mesh, in_specs=in_specs, out_specs=out_specs, check_vma=False)
```

```python
import functools
import math

import jax
import jax.numpy as jnp
from jax import lax
from jax.experimental import pallas as pl
from jax.experimental.pallas import tpu as pltpu
from jax.sharding import PartitionSpec as P

HOPS = 2
MESH = pl.DeviceIdType.MESH
TEMPER = 3.0
BIAS = -4.0

F32 = jnp.float32
BF16 = jnp.bfloat16
LIFT = 2.0**48
LOG2E = 1.4426950408889634
LN2 = 0.6931471805599453


def log1p_of(x):
    return jnp.where(x < 1e-3, x * (1.0 - 0.5 * x), jnp.log(1.0 + x))


def join(a, b):
    return a + b + a * b


def code(x):
    x = x * LIFT
    return (x * jnp.abs(x)).astype(BF16)


def decode(y):
    y = y.astype(F32)
    x = jnp.sqrt(jnp.abs(y)) * (1.0 / LIFT)
    return jnp.where(y < 0, -x, x)


def by_rows(n, step, body):
    def at(i, carry):
        body(pl.multiple_of(i * step, step))
        return carry

    lax.fori_loop(0, n // step, at, 0)


def kernel(
    n_dp, n_parts, scale, img, txt, iid, tid, loss_o, gi_o, gt_o,
    X, ST, IDS, SID, GV, GS, CS, CV, YS, YR, XS, RX, LV, LS, LOS, LOR, LFIN,
    xs, xr, cs, cr, ys, yr, ids_s, ids_r, gs_s, gs_r, rs, rr, cvs, cvr, os, orr, los, lor,
):
    WD, R = img.shape
    H = R // 2
    C = R // n_parts
    NH = n_parts // 2
    N_PIECES = R // 128
    PER = C // 128
    KW = 2 * WD
    STEP = 96
    d = lax.axis_index("dp")
    f = lax.axis_index("feat")
    n_cell = n_dp // 2
    c = d // 2
    a = lax.rem(d, 2)
    flip = c // (n_cell // 2)
    role = lax.rem(f + flip, 2)
    other = 1 - f
    c_next = lax.rem(c + 1, n_cell)
    c_last = lax.rem(c + n_cell - 1, n_cell)
    f_next = lax.rem(role + c_next // (n_cell // 2), 2)
    f_last = lax.rem(role + c_last // (n_cell // 2), 2)
    partner = (d, other)
    core = (2 * c + 1 - a, f)
    diag = (2 * c + 1 - a, other)

    def nxt(core_index):
        return (2 * c_next + core_index, f_next)

    def last(core_index):
        return (2 * c_last + core_index, f_last)

    own_at = pl.multiple_of(f * WD, WD)
    oth_at = pl.multiple_of(other * WD, WD)
    own_half, oth_half = pl.ds(own_at, WD), pl.ds(oth_at, WD)
    a_part = pl.ds(pl.multiple_of(a * H, H), H)

    def chunk(j):
        return pl.ds(pl.multiple_of(j * C, C), C) if not isinstance(j, int) else pl.ds(j * C, C)

    def piece(q):
        return pl.ds(pl.multiple_of(q * 128, 128), 128) if not isinstance(q, int) else pl.ds(q * 128, 128)

    def rcopy(src, dst, ssem, rsem, dev):
        return pltpu.make_async_remote_copy(
            src_ref=src, dst_ref=dst, send_sem=ssem, recv_sem=rsem, device_id=dev, device_id_type=MESH
        )

    def got(dst, rsem):
        pltpu.make_async_copy(dst, dst, rsem).wait()

    def sent(src, ssem):
        pltpu.make_async_copy(src, src, ssem).wait()

    barrier = pltpu.get_barrier_semaphore()
    near = (partner, core, diag)

    def arrive(far, senders):
        for dev in (*near, far):
            pl.semaphore_signal(barrier, inc=1, device_id=dev, device_id_type=MESH)
        pl.when(a == senders)(lambda: pl.semaphore_wait(barrier, len(near) + 2))
        pl.when(a != senders)(lambda: pl.semaphore_wait(barrier, len(near)))

    raws = (img, txt)

    def send_raw(kind, slot):
        raw = raws[kind]
        for j in range(n_parts):
            rcopy(raw.at[:, chunk(j)], X.at[slot, own_half, chunk(j)], xs.at[kind, j], xr.at[kind, j], partner).start()

    def raw_sent(kind):
        for j in range(n_parts):
            sent(raws[kind].at[:, chunk(j)], xs.at[kind, j])

    def place(kind, slot):
        def some(i):
            X[slot, pl.ds(pl.multiple_of(own_at + i, STEP), STEP), :] = raws[kind][pl.ds(i, STEP), :]

        by_rows(WD, STEP, some)

    def assemble(kind, slot, j):
        got(X.at[slot, oth_half, chunk(j)], xr.at[kind, j])

    def whole(slot, j):
        return X.at[slot, :, chunk(j)]

    def to_core(slot, j):
        rcopy(whole(slot, j), whole(slot, j), cs.at[slot, j], cr.at[slot, j], core).start()

    def from_core(slot, j):
        got(whole(slot, j), cr.at[slot, j])

    def to_core_sent(slot, j):
        sent(whole(slot, j), cs.at[slot, j])

    def move(slot, j, dev):
        rcopy(whole(slot, j), whole(3, j), ys.at[j], yr.at[j], dev).start()

    def ids_to_core(slot):
        rcopy(IDS.at[slot], IDS.at[slot], ids_s.at[slot], ids_r.at[slot], core).start()

    def ids_move(slot, k, dev):
        rcopy(IDS.at[slot], IDS.at[3], ids_s.at[3 + k], ids_r.at[3], dev).start()

    def ids_of(slot):
        got(IDS.at[slot], ids_r.at[slot])

    def column(s_acc, slot):
        for j in range(n_parts):
            row = IDS[slot, 0:1, chunk(j)]
            SID[s_acc, chunk(j), :] = jnp.transpose(jnp.broadcast_to(row, (128, C)))

    def turned(s_acc, j, image_rows):
        if image_rows and s_acc == 0:
            return pl.ds(0, C)
        return pl.ds(pl.multiple_of(C + j * C, C), C)

    def units(jobs, image_rows, first):
        rights = [X[s_slot, :, chunk(j)] for _, _, _, s_slot, j in jobs]
        lefts = [X[v_slot, :, a_part] for _, v_slot, _, _, _ in jobs]
        if first:
            done = []
            for (_, _, s_acc, s_slot, j), right in zip(jobs, rights):
                if s_slot not in done:
                    ST[turned(s_acc, j, image_rows), :] = jnp.transpose(right)
                    done.append(s_slot)
        scores = [
            jnp.dot(ST[turned(s_acc, j, image_rows), :], left, preferred_element_type=F32)
            for (_, _, s_acc, _, j), left in zip(jobs, lefts)
        ]
        v_sums, s_sums = {}, {}
        for (v, v_slot, s_acc, _, j), right, left, score in zip(jobs, rights, lefts, scores):
            logits = (scale * LOG2E) * score + BIAS * LOG2E
            sid = jnp.concatenate([SID[s_acc, chunk(j), :]] * (H // 128), axis=1)
            same = sid == IDS[v_slot, 0:1, a_part]
            e = jnp.exp2(-jnp.abs(logits))
            den = 1.0 + e
            inv = pl.reciprocal(den, approx=True)
            inv = inv * (2.0 - den * inv)
            z = jnp.where(same, -logits, logits)
            sig = jnp.where(z >= 0, inv, e * inv)
            w = jnp.where(same, -sig, sig).astype(BF16)
            total, prod = jnp.maximum(z, 0.0), e
            if image_rows:
                while total.shape[0] > 8:
                    n = total.shape[0] // 2
                    total = total[:n] + total[n:]
                    prod = join(prod[:n], prod[n:])
                LV[v] += LN2 * total + log1p_of(prod)
            else:
                while total.shape[1] > 128:
                    n = total.shape[1] // 2
                    total = total[:, :n] + total[:, n:]
                    prod = join(prod[:, :n], prod[:, n:])
                LS[0, chunk(j), :] += total
                LS[1, chunk(j), :] = join(LS[1, chunk(j), :], prod)
            v_part = jnp.dot(right, w, preferred_element_type=F32)
            v_sums[v] = v_sums[v] + v_part if v in v_sums else v_part
            s_part_of = lax.dot_general(left, w, (((1,), (1,)), ((), ())), preferred_element_type=F32)
            at = (s_acc, id(j))
            s_sums[at] = ((s_acc, j), s_sums[at][1] + s_part_of if at in s_sums else s_part_of)
        for v, value in v_sums.items():
            GV[v] += value
        for (s_acc, j), value in s_sums.values():
            if first:
                GS[s_acc, :, chunk(j)] = value
            else:
                GS[s_acc, :, chunk(j)] += value

    def rows_at(base, i):
        return pl.ds(pl.multiple_of(base + i, STEP), STEP)

    def staged(b, q):
        return piece(b * (N_PIECES // 2) + q)

    def give(b, q, value, kind, dst, dev):
        def some(i):
            XS[pl.ds(i, STEP), staged(b, q)] = code(scale * value(rows_at(oth_at, i)))

        by_rows(WD, STEP, some)
        rcopy(XS.at[:, staged(b, q)], RX.at[kind, :, piece(dst)], os.at[b, q], orr.at[kind, dst], dev).start()

    def given(b, n):
        def one(q, carry):
            sent(XS.at[:, staged(b, q)], os.at[b, q])
            return carry

        lax.fori_loop(0, n, one, 0)

    def keep(out, q, value, plus=False):
        def some(i):
            mine = scale * value(rows_at(own_at, i))
            out[pl.ds(i, STEP), piece(q)] = out[pl.ds(i, STEP), piece(q)] + mine if plus else mine

        by_rows(WD, STEP, some)

    def taken(out, kind, q, plus):
        got(RX.at[kind, :, piece(q)], orr.at[kind, q])

        def some(i):
            value = decode(RX[kind, pl.ds(i, STEP), piece(q)])
            out[pl.ds(i, STEP), piece(q)] = out[pl.ds(i, STEP), piece(q)] + value if plus else value

        by_rows(WD, STEP, some)

    def taken_from_both(out, kind, plus):
        def one(q):
            taken(out, kind, q, plus)
            taken(out, kind, N_PIECES // 2 + q, plus)

        over(N_PIECES // 2, one)

    def over(n, body):
        def one(q, carry):
            body(q)
            return carry

        lax.fori_loop(0, n, one, 0)

    def turn_back(v, dev):
        def one(q):
            def some(i):
                YS[pl.ds(i, STEP), piece(q)] = code(GV[v, pl.ds(i, STEP), piece(q)])

            by_rows(KW, STEP, some)
            rcopy(YS.at[:, piece(q)], YR.at[:, piece(q)], rs.at[q], rr.at[q], dev).start()

        over(N_PIECES // 2, one)

    def turned_back():
        over(N_PIECES // 2, lambda q: sent(YS.at[:, piece(q)], rs.at[q]))

    def v_value(v, q):
        return lambda rows: GV[v, rows, piece(q)]

    def with_returned(v, q):
        got(YR.at[:, piece(q)], rr.at[q])
        return lambda rows: GV[v, rows, piece(q)] + decode(YR[rows, piece(q)])

    def cv_send(q, value):
        def some(i):
            CV[0, pl.ds(i, STEP), piece(q)] = scale * value(rows_at(own_at, i))

        by_rows(WD, STEP, some)
        rcopy(CV.at[0, :, piece(q)], CV.at[1, :, piece(q)], cvs.at[q], cvr.at[q], core).start()

    def cv_keep(out, base, plus=False):
        def one(q):
            got(CV.at[1, :, piece(q)], cvr.at[q])

            def some(i):
                mine = CV[1, pl.ds(i, STEP), piece(q)]
                at = (pl.ds(i, STEP), piece(base + q))
                out[at] = out[at] + mine if plus else mine

            by_rows(WD, STEP, some)

        over(N_PIECES // 2, one)

    def cv_sent():
        over(N_PIECES // 2, lambda q: sent(CV.at[0, :, piece(q)], cvs.at[q]))

    def s_part(s_acc, j):
        rcopy(GS.at[s_acc, :, chunk(j)], CS.at[:, chunk(j)], gs_s.at[j], gs_r.at[j], core).start()

    def s_part_sent(s_acc):
        for j in range(n_parts):
            sent(GS.at[s_acc, :, chunk(j)], gs_s.at[j])

    def s_home(s_acc, j, out, b, kind, dev):
        got(CS.at[:, chunk(j)], gs_r.at[j])

        def one(i):
            q = j * PER + i

            def value(rows):
                return GS[s_acc, rows, piece(q)] + CS[rows, piece(q)]

            give(b, q, value, kind, q, dev)
            keep(out, q, value)

        over(PER, one)

    def zero():
        def some(i):
            for v in range(3):
                GV[v, pl.ds(i, STEP), :] = jnp.zeros((STEP, H), F32)

        by_rows(KW, STEP, some)
        LV[...] = jnp.zeros_like(LV)

    def zero_rows():
        def some(i):
            LS[:, pl.ds(i, C), :] = jnp.zeros((2, C, 128), F32)

        by_rows(R, C, some)

    def row_of(v):
        return jnp.broadcast_to(jnp.sum(LV[v], axis=0, keepdims=True), (8, H))

    def row_of_s(start):
        col = LN2 * LS[0, start : start + H, :] + log1p_of(LS[1, start : start + H, :])
        row = jnp.sum(jnp.transpose(col), axis=0, keepdims=True)
        return jnp.broadcast_to(row, (8, H))

    mean = 1.0 / float((HOPS + 1) * R)

    def loss_out():
        loss_o[...] = LFIN[0:1, :] * mean

    def loss_to_partner():
        rcopy(LFIN, LFIN, los.at[3], lor.at[3], partner).start()

    def role_0():
        arrive(nxt(0), 0)

        @pl.when(a == 0)
        def _():
            send_raw(1, 1)
            IDS[0] = jnp.broadcast_to(iid[...], (8, R))
            IDS[1] = jnp.broadcast_to(tid[...], (8, R))
            ids_to_core(0)
            ids_to_core(1)
            ids_move(0, 0, last(0))
            ids_move(0, 1, last(1))
            place(0, 0)
            place(1, 1)

        @pl.when(a == 1)
        def _():
            send_raw(1, 2)
            send_raw(0, 0)
            IDS[2] = jnp.broadcast_to(tid[...], (8, R))
            ids_to_core(2)
            place(1, 2)

        zero()

        @pl.when(a == 0)
        def _():
            ids_of(2)
            ids_of(3)
            column(0, 2)
            column(1, 1)
            for j in range(n_parts):
                assemble(0, 0, j)
                if j >= NH:
                    to_core(0, j)
                move(0, j, last(j // NH))

        @pl.when(a == 1)
        def _():
            ids_of(0)
            ids_of(1)
            ids_of(3)
            column(0, 2)
            column(1, 1)
            for j in range(n_parts):
                assemble(1, 2, j)
                to_core(2, j)

        @pl.when(a == 1)
        def _():
            for j in range(NH, n_parts):
                from_core(0, j)

        for k in range(NH):
            got(whole(3, a * NH + k), yr.at[a * NH + k])

        def first(j, carry):
            @pl.when(a == 0)
            def _():
                assemble(1, 1, j)
                to_core(1, j)
                from_core(2, j)

            pl.when(a == 1)(lambda: from_core(1, j))
            units([(1, 3, 0, 2, j), (1, 3, 1, 1, j)], True, True)
            pl.when(a == 0)(lambda: s_part(0, j))

            @pl.when((a == 1) & (j > 0))
            def _():
                s_home(0, j - 1, gt_o, 1, 1, partner)

            return carry

        lax.fori_loop(0, n_parts, first, 0)
        turn_back(1, nxt(a))
        pl.when(a == 1)(lambda: s_home(0, n_parts - 1, gt_o, 1, 1, partner))

        def second(i, carry):
            j = 2 * i
            units([(0, 0, 1, 1, j), (0, 0, 1, 1, j + 1)], True, False)

            @pl.when(a == 1)
            def _():
                s_part(1, j)
                s_part(1, j + 1)

            @pl.when((a == 0) & (i > 0))
            def _():
                s_home(1, j - 2, gt_o, 1, 1, partner)
                s_home(1, j - 1, gt_o, 1, 1, partner)

            return carry

        lax.fori_loop(0, NH, second, 0)
        LOS[0] = row_of(0)
        LOS[1] = row_of(1)
        rcopy(LOS.at[1], LOR.at[1 + a], los.at[1], lor.at[1 + a], nxt(0)).start()

        @pl.when(a == 1)
        def _():
            rcopy(LOS.at[0], LOR.at[0], los.at[0], lor.at[0], core).start()

        @pl.when(a == 0)
        def _():
            s_home(1, n_parts - 2, gt_o, 1, 1, partner)
            s_home(1, n_parts - 1, gt_o, 1, 1, partner)
            for i in range(3):
                got(LOR.at[i], lor.at[i])
            LFIN[:, 0:H] = LOS[0] + LOR[1]
            LFIN[:, H:R] = LOR[0] + LOR[2]
            loss_to_partner()
            loss_out()

            def one(q):
                value = with_returned(0, q)
                give(0, q, value, 0, q, partner)
                keep(gi_o, q, value)
                taken(gt_o, 1, q, True)
                taken(gt_o, 1, N_PIECES // 2 + q, True)

            over(N_PIECES // 2, one)
            cv_keep(gi_o, N_PIECES // 2)
            raw_sent(1)
            for j in range(n_parts):
                to_core_sent(1, j)
                sent(whole(0, j), ys.at[j])
            for j in range(NH, n_parts):
                to_core_sent(0, j)
            for k in (0, 1, 3, 4):
                sent(IDS.at[0], ids_s.at[k])
            s_part_sent(0)
            sent(LFIN, los.at[3])

        @pl.when(a == 1)
        def _():
            def one(q):
                value = with_returned(0, q)
                give(0, q, value, 0, N_PIECES // 2 + q, diag)
                cv_send(q, value)
                taken(gi_o, 0, 2 * q, False)
                taken(gi_o, 0, 2 * q + 1, False)

            over(N_PIECES // 2, one)
            got(LFIN, lor.at[3])
            loss_out()
            taken_from_both(gt_o, 1, True)
            raw_sent(0)
            raw_sent(1)
            for j in range(n_parts):
                to_core_sent(2, j)
            sent(IDS.at[2], ids_s.at[2])
            s_part_sent(1)
            sent(LOS.at[0], los.at[0])
            cv_sent()

        given(0, N_PIECES // 2)
        given(1, N_PIECES)
        sent(LOS.at[1], los.at[1])
        turned_back()

    def role_1():
        arrive(last(1), 1)

        @pl.when(a == 0)
        def _():
            send_raw(0, 0)
            send_raw(1, 1)
            IDS[1] = jnp.broadcast_to(tid[...], (8, R))
            ids_to_core(1)
            place(1, 1)

        @pl.when(a == 1)
        def _():
            send_raw(1, 2)
            IDS[0] = jnp.broadcast_to(iid[...], (8, R))
            IDS[2] = jnp.broadcast_to(tid[...], (8, R))
            ids_to_core(0)
            ids_to_core(2)
            ids_move(2, 0, nxt(0))
            ids_move(2, 1, nxt(1))
            place(1, 2)
            place(0, 0)

        zero()
        zero_rows()

        @pl.when(a == 0)
        def _():
            ids_of(0)
            ids_of(2)
            ids_of(3)
            column(0, 0)
            for j in range(n_parts):
                assemble(1, 1, j)
                if j >= NH:
                    to_core(1, j)
            for j in range(NH):
                from_core(2, j)

        @pl.when(a == 1)
        def _():
            ids_of(1)
            ids_of(3)
            column(0, 0)
            for j in range(n_parts):
                assemble(1, 2, j)
                if j < NH:
                    to_core(2, j)
                move(2, j, nxt(j // NH))
            for j in range(NH, n_parts):
                from_core(1, j)

        def step(j, carry):
            @pl.when(a == 1)
            def _():
                assemble(0, 0, j)
                to_core(0, j)

            pl.when(a == 0)(lambda: from_core(0, j))
            units([(0, 2, 0, 0, j), (1, 1, 0, 0, j)], False, True)
            return carry

        lax.fori_loop(0, n_parts, step, 0)

        @pl.when(a == 0)
        def _():
            def own(q):
                give(1, q, v_value(1, q), 1, q, partner)
                keep(gt_o, q, v_value(1, q))

            over(N_PIECES // 2, own)

        @pl.when(a == 1)
        def _():
            def own(q):
                give(1, q, v_value(1, q), 1, N_PIECES // 2 + q, diag)
                cv_send(q, v_value(1, q))

            over(N_PIECES // 2, own)

        for k in range(NH):
            got(whole(3, a * NH + k), yr.at[a * NH + k])

        def final(i, carry):
            j = 2 * i
            units([(2, 3, 0, 0, j), (2, 3, 0, 0, j + 1)], False, False)

            @pl.when(a == 0)
            def _():
                s_part(0, j)
                s_part(0, j + 1)

            @pl.when((a == 1) & (i > 0))
            def _():
                s_home(0, j - 2, gi_o, 2, 0, partner)
                s_home(0, j - 1, gi_o, 2, 0, partner)

            return carry

        lax.fori_loop(0, NH, final, 0)
        turn_back(2, last(a))

        @pl.when(a == 0)
        def _():
            LOS[0] = row_of_s(0)
            LOS[1] = row_of_s(H)
            for i in range(2):
                rcopy(LOS.at[i], LOR.at[i], los.at[i], lor.at[i], core).start()

            def one(q):
                value = with_returned(0, q)
                give(0, q, value, 1, q, diag)
                cv_send(q, value)
                taken(gt_o, 1, 2 * q, True)
                taken(gt_o, 1, 2 * q + 1, True)

            cv_keep(gt_o, N_PIECES // 2)
            over(N_PIECES // 2, one)
            got(LFIN, lor.at[3])
            loss_out()
            taken_from_both(gi_o, 0, False)
            raw_sent(0)
            raw_sent(1)
            for j in range(NH, n_parts):
                to_core_sent(1, j)
            sent(IDS.at[1], ids_s.at[1])
            s_part_sent(0)
            for i in range(2):
                sent(LOS.at[i], los.at[i])

        @pl.when(a == 1)
        def _():
            s_home(0, n_parts - 2, gi_o, 2, 0, partner)
            s_home(0, n_parts - 1, gi_o, 2, 0, partner)
            for i in range(2):
                got(LOR.at[i], lor.at[i])
                LFIN[:, i * H : (i + 1) * H] = row_of_s(i * H) + LOR[i]
            loss_to_partner()
            loss_out()

            def one(q):
                value = with_returned(0, q)
                give(0, q, value, 1, N_PIECES // 2 + q, partner)
                keep(gt_o, N_PIECES // 2 + q, value, plus=True)

            over(N_PIECES, lambda q: taken(gt_o, 1, q, False))
            over(N_PIECES // 2, one)
            cv_keep(gt_o, 0, plus=True)
            raw_sent(1)
            for j in range(n_parts):
                to_core_sent(0, j)
                sent(whole(2, j), ys.at[j])
            for j in range(NH):
                to_core_sent(2, j)
            for k in (0, 2, 3, 4):
                sent(IDS.at[0], ids_s.at[k])
            given(2, N_PIECES)
            sent(LFIN, los.at[3])

        given(0, N_PIECES // 2)
        given(1, N_PIECES // 2)
        turned_back()
        cv_sent()

    pl.when(role == 0)(role_0)
    pl.when(role == 1)(role_1)


def per_device(n_dp, n_parts, image_emb, text_emb, image_ids, text_ids):
    R, width = image_emb.shape
    H, C = R // 2, R // n_parts
    KW = 2 * width
    scale = TEMPER / math.sqrt(KW)
    ids = [i[None, :] for i in (image_ids, text_ids)]
    dma = pltpu.SemaphoreType.DMA
    vmem = pltpu.VMEM
    scratch = [
        vmem((4, KW, R), BF16),
        vmem((C + R, KW), BF16),
        vmem((4, 8, R), jnp.int32),
        vmem((2, R, 128), jnp.int32),
        vmem((3, KW, H), F32),
        vmem((2, KW, R), F32),
        vmem((KW, R), F32),
        vmem((2, width, H), F32),
        vmem((KW, H), BF16),
        vmem((KW, H), BF16),
        vmem((width, 2 * R), BF16),
        vmem((2, width, R), BF16),
        vmem((2, 8, H), F32),
        vmem((2, R, 128), F32),
        vmem((2, 8, H), F32),
        vmem((3, 8, H), F32),
        vmem((8, R), F32),
        dma((2, n_parts)), dma((2, n_parts)),
        dma((3, n_parts)), dma((3, n_parts)),
        dma((n_parts,)), dma((n_parts,)),
        dma((5,)), dma((4,)),
        dma((n_parts,)), dma((n_parts,)),
        dma((R // 256,)), dma((R // 256,)),
        dma((R // 256,)), dma((R // 256,)),
        dma((3, R // 128)), dma((2, R // 128)),
        dma((4,)), dma((4,)),
    ]
    flops = 9 * 2 * H * R * KW
    loss, grad_image, grad_text = pl.pallas_call(
        functools.partial(kernel, n_dp, n_parts, scale),
        out_shape=[
            pltpu.VMEM((1, R), F32),
            pltpu.VMEM((width, R), F32),
            pltpu.VMEM((width, R), F32),
        ],
        in_specs=[pl.BlockSpec(memory_space=vmem)] * 4,
        out_specs=[pl.BlockSpec(memory_space=vmem)] * 3,
        scratch_shapes=scratch,
        compiler_params=pltpu.CompilerParams(
            collective_id=0, has_side_effects=True, vmem_limit_bytes=56 * 2**20
        ),
        cost_estimate=pl.CostEstimate(flops=flops, bytes_accessed=12 * R * width, transcendentals=4 * H * R),
    )(image_emb.T, text_emb.T, *ids)
    return (loss[0], grad_image.T, grad_text.T)


def solution(mesh):
    in_specs = (P("dp", "feat"), P("dp", "feat"), P("dp"), P("dp"))
    out_specs = (P("dp"), P("dp", "feat"), P("dp", "feat"))
    body = functools.partial(per_device, mesh.shape["dp"], 4)
    return jax.shard_map(body, mesh=mesh, in_specs=in_specs, out_specs=out_specs, check_vma=False)
```

```python
import functools
import math

import jax
import jax.numpy as jnp
from jax import lax
from jax.experimental import pallas as pl
from jax.experimental.pallas import tpu as pltpu
from jax.sharding import PartitionSpec as P

HOPS = 2
MESH = pl.DeviceIdType.MESH
TEMPER = 3.0
BIAS = -4.0

F32 = jnp.float32
BF16 = jnp.bfloat16
LIFT = 2.0**48
LOG2E = 1.4426950408889634
LN2 = 0.6931471805599453


def log1p_of(x):
    return jnp.where(x < 1e-3, x * (1.0 - 0.5 * x), jnp.log(1.0 + x))


def join(a, b):
    return a + b + a * b


def code(x):
    x = x * LIFT
    return (x * jnp.abs(x)).astype(BF16)


def decode(y):
    y = y.astype(F32)
    x = jnp.sqrt(jnp.abs(y)) * (1.0 / LIFT)
    return jnp.where(y < 0, -x, x)


def by_rows(n, step, body):
    def at(i, carry):
        body(pl.multiple_of(i * step, step))
        return carry

    lax.fori_loop(0, n // step, at, 0)


def kernel(
    n_dp, n_parts, scale, img, txt, iid, tid, loss_o, gi_o, gt_o,
    X, ST, IDS, SID, GV, GS, CS, CV, YS, YR, XS, RX, LV, LS, LOS, LOR, LFIN,
    xs, xr, cs, cr, ys, yr, ids_s, ids_r, gs_s, gs_r, rs, rr, cvs, cvr, os, orr, los, lor, ready,
):
    WD, R = img.shape
    H = R // 2
    C = R // n_parts
    NH = n_parts // 2
    N_PIECES = R // 128
    PER = C // 128
    KW = 2 * WD
    STEP = 576
    d = lax.axis_index("dp")
    f = lax.axis_index("feat")
    n_cell = n_dp // 2
    c = d // 2
    a = lax.rem(d, 2)
    flip = c // (n_cell // 2)
    role = lax.rem(f + flip, 2)
    other = 1 - f
    c_next = lax.rem(c + 1, n_cell)
    c_last = lax.rem(c + n_cell - 1, n_cell)
    f_next = lax.rem(role + c_next // (n_cell // 2), 2)
    f_last = lax.rem(role + c_last // (n_cell // 2), 2)
    partner = (d, other)
    core = (2 * c + 1 - a, f)
    diag = (2 * c + 1 - a, other)

    def nxt(core_index):
        return (2 * c_next + core_index, f_next)

    def last(core_index):
        return (2 * c_last + core_index, f_last)

    own_at = pl.multiple_of(f * WD, WD)
    oth_at = pl.multiple_of(other * WD, WD)
    own_half, oth_half = pl.ds(own_at, WD), pl.ds(oth_at, WD)
    a_part = pl.ds(pl.multiple_of(a * H, H), H)

    def chunk(j):
        return pl.ds(pl.multiple_of(j * C, C), C) if not isinstance(j, int) else pl.ds(j * C, C)

    def piece(q):
        return pl.ds(pl.multiple_of(q * 128, 128), 128) if not isinstance(q, int) else pl.ds(q * 128, 128)

    def rcopy(src, dst, ssem, rsem, dev):
        return pltpu.make_async_remote_copy(
            src_ref=src, dst_ref=dst, send_sem=ssem, recv_sem=rsem, device_id=dev, device_id_type=MESH
        )

    def got(dst, rsem):
        pltpu.make_async_copy(dst, dst, rsem).wait()

    def sent(src, ssem):
        pltpu.make_async_copy(src, src, ssem).wait()

    barrier = pltpu.get_barrier_semaphore()
    near = (partner, core, diag)

    def arrive(far, senders):
        for dev in (*near, far):
            pl.semaphore_signal(barrier, inc=1, device_id=dev, device_id_type=MESH)

        @pl.when(a != senders)
        def _():
            pl.semaphore_wait(barrier, len(near))
            pl.semaphore_signal(ready, inc=1, device_id=partner, device_id_type=MESH)

        pl.when(a == senders)(lambda: pl.semaphore_wait(ready, 1))

    def neighbours_in():
        pl.semaphore_wait(barrier, len(near) + 2)

    raws = (img, txt)

    def send_raw(kind, slot):
        raw = raws[kind]
        for j in range(n_parts):
            rcopy(raw.at[:, chunk(j)], X.at[slot, own_half, chunk(j)], xs.at[kind, j], xr.at[kind, j], partner).start()

    def raw_sent(kind):
        for j in range(n_parts):
            sent(raws[kind].at[:, chunk(j)], xs.at[kind, j])

    def place(kind, slot):
        def some(i):
            X[slot, pl.ds(pl.multiple_of(own_at + i, STEP), STEP), :] = raws[kind][pl.ds(i, STEP), :]

        by_rows(WD, STEP, some)

    def assemble(kind, slot, j):
        got(X.at[slot, oth_half, chunk(j)], xr.at[kind, j])

    def whole(slot, j):
        return X.at[slot, :, chunk(j)]

    def to_core(slot, j):
        rcopy(whole(slot, j), whole(slot, j), cs.at[slot, j], cr.at[slot, j], core).start()

    def from_core(slot, j):
        got(whole(slot, j), cr.at[slot, j])

    def to_core_sent(slot, j):
        sent(whole(slot, j), cs.at[slot, j])

    def move_own(kind, j, dev):
        rcopy(raws[kind].at[:, chunk(j)], X.at[3, own_half, chunk(j)], ys.at[0, j], yr.at[0, j], dev).start()

    def move(slot, j, dev):
        rcopy(X.at[slot, oth_half, chunk(j)], X.at[3, oth_half, chunk(j)], ys.at[1, j], yr.at[1, j], dev).start()

    def move_sent(kind, slot, j):
        sent(raws[kind].at[:, chunk(j)], ys.at[0, j])
        sent(X.at[slot, oth_half, chunk(j)], ys.at[1, j])

    def moved_in(f_sender):
        for k in range(NH):
            j = a * NH + k
            for n, half in enumerate((f_sender, 1 - f_sender)):
                got(X.at[3, pl.ds(pl.multiple_of(half * WD, WD), WD), chunk(j)], yr.at[n, j])

    def ids_to_core(slot):
        rcopy(IDS.at[slot], IDS.at[slot], ids_s.at[slot], ids_r.at[slot], core).start()

    def ids_move(slot, k, dev):
        rcopy(IDS.at[slot], IDS.at[3], ids_s.at[3 + k], ids_r.at[3], dev).start()

    def ids_of(slot):
        got(IDS.at[slot], ids_r.at[slot])

    def column(s_acc, slot):
        for j in range(n_parts):
            row = IDS[slot, 0:1, chunk(j)]
            SID[s_acc, chunk(j), :] = jnp.transpose(jnp.broadcast_to(row, (128, C)))

    def turned(s_acc, j, image_rows):
        if image_rows and s_acc == 0:
            return pl.ds(0, C)
        return pl.ds(pl.multiple_of(C + j * C, C), C)

    def units(jobs, image_rows, first):
        rights = [X[s_slot, :, chunk(j)] for _, _, _, s_slot, j in jobs]
        lefts = [X[v_slot, :, a_part] for _, v_slot, _, _, _ in jobs]
        if first:
            done = []
            for (_, _, s_acc, s_slot, j), right in zip(jobs, rights):
                if s_slot not in done:
                    ST[turned(s_acc, j, image_rows), :] = jnp.transpose(right)
                    done.append(s_slot)
        scores = [
            jnp.dot(ST[turned(s_acc, j, image_rows), :], left, preferred_element_type=F32)
            for (_, _, s_acc, _, j), left in zip(jobs, lefts)
        ]
        v_sums, s_sums = {}, {}
        for (v, v_slot, s_acc, _, j), right, left, score in zip(jobs, rights, lefts, scores):
            logits = (scale * LOG2E) * score + BIAS * LOG2E
            sid = jnp.concatenate([SID[s_acc, chunk(j), :]] * (H // 128), axis=1)
            same = sid == IDS[v_slot, 0:1, a_part]
            e = jnp.exp2(-jnp.abs(logits))
            den = 1.0 + e
            inv = pl.reciprocal(den, approx=True)
            inv = inv * (2.0 - den * inv)
            z = jnp.where(same, -logits, logits)
            sig = jnp.where(z >= 0, inv, e * inv)
            w = jnp.where(same, -sig, sig).astype(BF16)
            total, prod = jnp.maximum(z, 0.0), e
            if image_rows:
                while total.shape[0] > 8:
                    n = total.shape[0] // 2
                    total = total[:n] + total[n:]
                    prod = join(prod[:n], prod[n:])
                LV[v] += LN2 * total + log1p_of(prod)
            else:
                while total.shape[1] > 128:
                    n = total.shape[1] // 2
                    total = total[:, :n] + total[:, n:]
                    prod = join(prod[:, :n], prod[:, n:])
                LS[0, chunk(j), :] += total
                LS[1, chunk(j), :] = join(LS[1, chunk(j), :], prod)
            v_part = jnp.dot(right, w, preferred_element_type=F32)
            v_sums[v] = v_sums[v] + v_part if v in v_sums else v_part
            s_part_of = lax.dot_general(left, w, (((1,), (1,)), ((), ())), preferred_element_type=F32)
            at = (s_acc, id(j))
            s_sums[at] = ((s_acc, j), s_sums[at][1] + s_part_of if at in s_sums else s_part_of)
        for v, value in v_sums.items():
            GV[v] += value
        for (s_acc, j), value in s_sums.values():
            if first:
                GS[s_acc, :, chunk(j)] = value
            else:
                GS[s_acc, :, chunk(j)] += value

    def rows_at(base, i):
        return pl.ds(pl.multiple_of(base + i, STEP), STEP)

    def staged(b, q):
        return piece(b * (N_PIECES // 2) + q)

    def give(b, q, value, kind, dst, dev):
        def some(i):
            XS[pl.ds(i, STEP), staged(b, q)] = code(scale * value(rows_at(oth_at, i)))

        by_rows(WD, STEP, some)
        rcopy(XS.at[:, staged(b, q)], RX.at[kind, :, piece(dst)], os.at[b, q], orr.at[kind, dst], dev).start()

    def given(b, n):
        def one(q, carry):
            sent(XS.at[:, staged(b, q)], os.at[b, q])
            return carry

        lax.fori_loop(0, n, one, 0)

    def keep(out, q, value, plus=False):
        def some(i):
            mine = scale * value(rows_at(own_at, i))
            out[pl.ds(i, STEP), piece(q)] = out[pl.ds(i, STEP), piece(q)] + mine if plus else mine

        by_rows(WD, STEP, some)

    def taken(out, kind, q, plus):
        got(RX.at[kind, :, piece(q)], orr.at[kind, q])

        def some(i):
            value = decode(RX[kind, pl.ds(i, STEP), piece(q)])
            out[pl.ds(i, STEP), piece(q)] = out[pl.ds(i, STEP), piece(q)] + value if plus else value

        by_rows(WD, STEP, some)

    def taken_from_both(out, kind, plus):
        def one(q):
            taken(out, kind, q, plus)
            taken(out, kind, N_PIECES // 2 + q, plus)

        over(N_PIECES // 2, one)

    def over(n, body):
        def one(q, carry):
            body(q)
            return carry

        lax.fori_loop(0, n, one, 0)

    def turn_back(v, dev):
        def one(q):
            def some(i):
                YS[pl.ds(i, STEP), piece(q)] = code(GV[v, pl.ds(i, STEP), piece(q)])

            by_rows(KW, STEP, some)
            rcopy(YS.at[:, piece(q)], YR.at[:, piece(q)], rs.at[q], rr.at[q], dev).start()

        over(N_PIECES // 2, one)

    def turned_back():
        over(N_PIECES // 2, lambda q: sent(YS.at[:, piece(q)], rs.at[q]))

    def v_value(v, q):
        return lambda rows: GV[v, rows, piece(q)]

    def with_returned(v, q):
        got(YR.at[:, piece(q)], rr.at[q])
        return lambda rows: GV[v, rows, piece(q)] + decode(YR[rows, piece(q)])

    def cv_send(q, value):
        def some(i):
            CV[0, pl.ds(i, STEP), piece(q)] = scale * value(rows_at(own_at, i))

        by_rows(WD, STEP, some)
        rcopy(CV.at[0, :, piece(q)], CV.at[1, :, piece(q)], cvs.at[q], cvr.at[q], core).start()

    def cv_keep(out, base, plus=False):
        def one(q):
            got(CV.at[1, :, piece(q)], cvr.at[q])

            def some(i):
                mine = CV[1, pl.ds(i, STEP), piece(q)]
                at = (pl.ds(i, STEP), piece(base + q))
                out[at] = out[at] + mine if plus else mine

            by_rows(WD, STEP, some)

        over(N_PIECES // 2, one)

    def cv_sent():
        over(N_PIECES // 2, lambda q: sent(CV.at[0, :, piece(q)], cvs.at[q]))

    def s_part(s_acc, j):
        rcopy(GS.at[s_acc, :, chunk(j)], CS.at[:, chunk(j)], gs_s.at[j], gs_r.at[j], core).start()

    def s_part_sent(s_acc):
        for j in range(n_parts):
            sent(GS.at[s_acc, :, chunk(j)], gs_s.at[j])

    def s_home(s_acc, j, out, b, kind, dev):
        got(CS.at[:, chunk(j)], gs_r.at[j])

        def one(i):
            q = j * PER + i

            def value(rows):
                return GS[s_acc, rows, piece(q)] + CS[rows, piece(q)]

            give(b, q, value, kind, q, dev)
            keep(out, q, value)

        over(PER, one)

    def zero():
        def some(i):
            for v in range(3):
                GV[v, pl.ds(i, STEP), :] = jnp.zeros((STEP, H), F32)

        by_rows(KW, STEP, some)
        LV[...] = jnp.zeros_like(LV)

    def zero_rows():
        def some(i):
            LS[:, pl.ds(i, C), :] = jnp.zeros((2, C, 128), F32)

        by_rows(R, C, some)

    def row_of(v):
        return jnp.broadcast_to(jnp.sum(LV[v], axis=0, keepdims=True), (8, H))

    def row_of_s(start):
        col = LN2 * LS[0, start : start + H, :] + log1p_of(LS[1, start : start + H, :])
        row = jnp.sum(jnp.transpose(col), axis=0, keepdims=True)
        return jnp.broadcast_to(row, (8, H))

    mean = 1.0 / float((HOPS + 1) * R)

    def loss_out():
        loss_o[...] = LFIN[0:1, :] * mean

    def loss_to_partner():
        rcopy(LFIN, LFIN, los.at[3], lor.at[3], partner).start()

    def role_0():
        arrive(nxt(0), 0)

        @pl.when(a == 0)
        def _():
            send_raw(1, 1)
            place(0, 0)
            place(1, 1)
            neighbours_in()
            IDS[0] = jnp.broadcast_to(iid[...], (8, R))
            IDS[1] = jnp.broadcast_to(tid[...], (8, R))
            ids_to_core(0)
            ids_to_core(1)
            ids_move(0, 0, last(0))
            ids_move(0, 1, last(1))
            for j in range(n_parts):
                move_own(0, j, last(j // NH))

        @pl.when(a == 1)
        def _():
            send_raw(1, 2)
            send_raw(0, 0)
            IDS[2] = jnp.broadcast_to(tid[...], (8, R))
            ids_to_core(2)
            place(1, 2)

        zero()

        @pl.when(a == 0)
        def _():
            ids_of(2)
            ids_of(3)
            column(0, 2)
            column(1, 1)
            for j in range(n_parts):
                assemble(0, 0, j)
                if j >= NH:
                    to_core(0, j)
                move(0, j, last(j // NH))

        @pl.when(a == 1)
        def _():
            ids_of(0)
            ids_of(1)
            ids_of(3)
            column(0, 2)
            column(1, 1)
            for j in range(n_parts):
                assemble(1, 2, j)
                to_core(2, j)

        @pl.when(a == 1)
        def _():
            for j in range(NH, n_parts):
                from_core(0, j)

        moved_in(f_next)

        def first(j, carry):
            @pl.when(a == 0)
            def _():
                assemble(1, 1, j)
                to_core(1, j)
                from_core(2, j)

            pl.when(a == 1)(lambda: from_core(1, j))
            units([(1, 3, 0, 2, j), (1, 3, 1, 1, j)], True, True)
            pl.when(a == 0)(lambda: s_part(0, j))

            @pl.when((a == 1) & (j > 0))
            def _():
                s_home(0, j - 1, gt_o, 1, 1, partner)

            return carry

        lax.fori_loop(0, n_parts, first, 0)
        turn_back(1, nxt(a))
        pl.when(a == 1)(lambda: s_home(0, n_parts - 1, gt_o, 1, 1, partner))

        def second(i, carry):
            j = 2 * i
            units([(0, 0, 1, 1, j), (0, 0, 1, 1, j + 1)], True, False)

            @pl.when(a == 1)
            def _():
                s_part(1, j)
                s_part(1, j + 1)

            @pl.when((a == 0) & (i > 0))
            def _():
                s_home(1, j - 2, gt_o, 1, 1, partner)
                s_home(1, j - 1, gt_o, 1, 1, partner)

            return carry

        lax.fori_loop(0, NH, second, 0)
        LOS[0] = row_of(0)
        LOS[1] = row_of(1)
        rcopy(LOS.at[1], LOR.at[1 + a], los.at[1], lor.at[1 + a], nxt(0)).start()

        @pl.when(a == 1)
        def _():
            rcopy(LOS.at[0], LOR.at[0], los.at[0], lor.at[0], core).start()

        @pl.when(a == 0)
        def _():
            s_home(1, n_parts - 2, gt_o, 1, 1, partner)
            s_home(1, n_parts - 1, gt_o, 1, 1, partner)

            def one(q):
                value = with_returned(0, q)
                give(0, q, value, 0, q, partner)
                keep(gi_o, q, value)

            over(N_PIECES // 2, one)
            for i in range(3):
                got(LOR.at[i], lor.at[i])
            LFIN[:, 0:H] = LOS[0] + LOR[1]
            LFIN[:, H:R] = LOR[0] + LOR[2]
            loss_to_partner()
            loss_out()
            taken_from_both(gt_o, 1, True)
            cv_keep(gi_o, N_PIECES // 2)
            raw_sent(1)
            for j in range(n_parts):
                to_core_sent(1, j)
                move_sent(0, 0, j)
            for j in range(NH, n_parts):
                to_core_sent(0, j)
            for k in (0, 1, 3, 4):
                sent(IDS.at[0], ids_s.at[k])
            s_part_sent(0)
            sent(LFIN, los.at[3])

        @pl.when(a == 1)
        def _():
            def one(q):
                value = with_returned(0, q)
                give(0, q, value, 0, N_PIECES // 2 + q, diag)
                cv_send(q, value)
                taken(gi_o, 0, 2 * q, False)
                taken(gi_o, 0, 2 * q + 1, False)

            over(N_PIECES // 2, one)
            got(LFIN, lor.at[3])
            loss_out()
            taken_from_both(gt_o, 1, True)
            raw_sent(0)
            raw_sent(1)
            for j in range(n_parts):
                to_core_sent(2, j)
            sent(IDS.at[2], ids_s.at[2])
            s_part_sent(1)
            sent(LOS.at[0], los.at[0])
            cv_sent()

        given(0, N_PIECES // 2)
        given(1, N_PIECES)
        sent(LOS.at[1], los.at[1])
        turned_back()

    def role_1():
        arrive(last(1), 1)

        @pl.when(a == 0)
        def _():
            send_raw(0, 0)
            send_raw(1, 1)
            IDS[1] = jnp.broadcast_to(tid[...], (8, R))
            ids_to_core(1)
            place(1, 1)

        @pl.when(a == 1)
        def _():
            send_raw(1, 2)
            place(1, 2)
            place(0, 0)
            neighbours_in()
            IDS[0] = jnp.broadcast_to(iid[...], (8, R))
            IDS[2] = jnp.broadcast_to(tid[...], (8, R))
            ids_to_core(0)
            ids_to_core(2)
            ids_move(2, 0, nxt(0))
            ids_move(2, 1, nxt(1))
            for j in range(n_parts):
                move_own(1, j, nxt(j // NH))

        zero()
        zero_rows()

        @pl.when(a == 0)
        def _():
            ids_of(0)
            ids_of(2)
            ids_of(3)
            column(0, 0)
            for j in range(n_parts):
                assemble(1, 1, j)
                if j >= NH:
                    to_core(1, j)
            for j in range(NH):
                from_core(2, j)

        @pl.when(a == 1)
        def _():
            ids_of(1)
            ids_of(3)
            column(0, 0)
            for j in range(n_parts):
                assemble(1, 2, j)
                if j < NH:
                    to_core(2, j)
                move(2, j, nxt(j // NH))
            for j in range(NH, n_parts):
                from_core(1, j)

        def step(j, carry):
            @pl.when(a == 1)
            def _():
                assemble(0, 0, j)
                to_core(0, j)

            pl.when(a == 0)(lambda: from_core(0, j))
            units([(0, 2, 0, 0, j), (1, 1, 0, 0, j)], False, True)
            return carry

        lax.fori_loop(0, n_parts, step, 0)

        @pl.when(a == 0)
        def _():
            def own(q):
                give(1, q, v_value(1, q), 1, q, partner)
                keep(gt_o, q, v_value(1, q))

            over(N_PIECES // 2, own)

        @pl.when(a == 1)
        def _():
            def own(q):
                give(1, q, v_value(1, q), 1, N_PIECES // 2 + q, diag)
                cv_send(q, v_value(1, q))

            over(N_PIECES // 2, own)

        moved_in(f_last)

        def final(i, carry):
            j = 2 * i
            units([(2, 3, 0, 0, j), (2, 3, 0, 0, j + 1)], False, False)

            @pl.when(a == 0)
            def _():
                s_part(0, j)
                s_part(0, j + 1)

            @pl.when((a == 1) & (i > 0))
            def _():
                s_home(0, j - 2, gi_o, 2, 0, partner)
                s_home(0, j - 1, gi_o, 2, 0, partner)

            return carry

        lax.fori_loop(0, NH, final, 0)
        turn_back(2, last(a))

        @pl.when(a == 0)
        def _():
            LOS[0] = row_of_s(0)
            LOS[1] = row_of_s(H)
            for i in range(2):
                rcopy(LOS.at[i], LOR.at[i], los.at[i], lor.at[i], core).start()

            def one(q):
                value = with_returned(0, q)
                give(0, q, value, 1, q, diag)
                cv_send(q, value)
                taken(gt_o, 1, 2 * q, True)
                taken(gt_o, 1, 2 * q + 1, True)

            cv_keep(gt_o, N_PIECES // 2)
            over(N_PIECES // 2, one)
            got(LFIN, lor.at[3])
            loss_out()
            taken_from_both(gi_o, 0, False)
            raw_sent(0)
            raw_sent(1)
            for j in range(NH, n_parts):
                to_core_sent(1, j)
            sent(IDS.at[1], ids_s.at[1])
            s_part_sent(0)
            for i in range(2):
                sent(LOS.at[i], los.at[i])

        @pl.when(a == 1)
        def _():
            s_home(0, n_parts - 2, gi_o, 2, 0, partner)
            s_home(0, n_parts - 1, gi_o, 2, 0, partner)
            for i in range(2):
                got(LOR.at[i], lor.at[i])
                LFIN[:, i * H : (i + 1) * H] = row_of_s(i * H) + LOR[i]
            loss_to_partner()
            loss_out()

            def one(q):
                value = with_returned(0, q)
                give(0, q, value, 1, N_PIECES // 2 + q, partner)
                keep(gt_o, N_PIECES // 2 + q, value, plus=True)

            over(N_PIECES, lambda q: taken(gt_o, 1, q, False))
            over(N_PIECES // 2, one)
            cv_keep(gt_o, 0, plus=True)
            raw_sent(1)
            for j in range(n_parts):
                to_core_sent(0, j)
                move_sent(1, 2, j)
            for j in range(NH):
                to_core_sent(2, j)
            for k in (0, 2, 3, 4):
                sent(IDS.at[0], ids_s.at[k])
            given(2, N_PIECES)
            sent(LFIN, los.at[3])

        given(0, N_PIECES // 2)
        given(1, N_PIECES // 2)
        turned_back()
        cv_sent()

    pl.when(role == 0)(role_0)
    pl.when(role == 1)(role_1)


def per_device(n_dp, n_parts, image_emb, text_emb, image_ids, text_ids):
    R, width = image_emb.shape
    H, C = R // 2, R // n_parts
    KW = 2 * width
    scale = TEMPER / math.sqrt(KW)
    ids = [i[None, :] for i in (image_ids, text_ids)]
    dma = pltpu.SemaphoreType.DMA
    vmem = pltpu.VMEM
    scratch = [
        vmem((4, KW, R), BF16),
        vmem((C + R, KW), BF16),
        vmem((4, 8, R), jnp.int32),
        vmem((2, R, 128), jnp.int32),
        vmem((3, KW, H), F32),
        vmem((2, KW, R), F32),
        vmem((KW, R), F32),
        vmem((2, width, H), F32),
        vmem((KW, H), BF16),
        vmem((KW, H), BF16),
        vmem((width, 2 * R), BF16),
        vmem((2, width, R), BF16),
        vmem((2, 8, H), F32),
        vmem((2, R, 128), F32),
        vmem((2, 8, H), F32),
        vmem((3, 8, H), F32),
        vmem((8, R), F32),
        dma((2, n_parts)), dma((2, n_parts)),
        dma((3, n_parts)), dma((3, n_parts)),
        dma((2, n_parts)), dma((2, n_parts)),
        dma((5,)), dma((4,)),
        dma((n_parts,)), dma((n_parts,)),
        dma((R // 256,)), dma((R // 256,)),
        dma((R // 256,)), dma((R // 256,)),
        dma((3, R // 128)), dma((2, R // 128)),
        dma((4,)), dma((4,)),
        pltpu.SemaphoreType.REGULAR,
    ]
    flops = 9 * 2 * H * R * KW
    loss, grad_image, grad_text = pl.pallas_call(
        functools.partial(kernel, n_dp, n_parts, scale),
        out_shape=[
            pltpu.VMEM((1, R), F32),
            pltpu.VMEM((width, R), F32),
            pltpu.VMEM((width, R), F32),
        ],
        in_specs=[pl.BlockSpec(memory_space=vmem)] * 4,
        out_specs=[pl.BlockSpec(memory_space=vmem)] * 3,
        scratch_shapes=scratch,
        compiler_params=pltpu.CompilerParams(
            collective_id=0, has_side_effects=True, vmem_limit_bytes=56 * 2**20
        ),
        cost_estimate=pl.CostEstimate(flops=flops, bytes_accessed=12 * R * width, transcendentals=4 * H * R),
    )(image_emb.T, text_emb.T, *ids)
    return (loss[0], grad_image.T, grad_text.T)


def solution(mesh):
    in_specs = (P("dp", "feat"), P("dp", "feat"), P("dp"), P("dp"))
    out_specs = (P("dp"), P("dp", "feat"), P("dp", "feat"))
    body = functools.partial(per_device, mesh.shape["dp"], 4)
    return jax.shard_map(body, mesh=mesh, in_specs=in_specs, out_specs=out_specs, check_vma=False)
```

```python
import functools
import math

import jax
import jax.numpy as jnp
from jax import lax
from jax.experimental import pallas as pl
from jax.experimental.pallas import tpu as pltpu
from jax.sharding import PartitionSpec as P

HOPS = 2
MESH = pl.DeviceIdType.MESH
TEMPER = 3.0
BIAS = -4.0

F32 = jnp.float32
BF16 = jnp.bfloat16
LIFT = 2.0**48
LOG2E = 1.4426950408889634
LN2 = 0.6931471805599453


def log1p_of(x):
    return jnp.where(x < 1e-3, x * (1.0 - 0.5 * x), jnp.log(1.0 + x))


def join(a, b):
    return a + b + a * b


def code(x):
    x = x * LIFT
    return (x * jnp.abs(x)).astype(BF16)


def decode(y):
    y = y.astype(F32)
    x = jnp.sqrt(jnp.abs(y)) * (1.0 / LIFT)
    return jnp.where(y < 0, -x, x)


def by_rows(n, step, body):
    def at(i, carry):
        body(pl.multiple_of(i * step, step))
        return carry

    lax.fori_loop(0, n // step, at, 0)


def kernel(
    n_dp, n_parts, scale, img, txt, iid, tid, loss_o, gi_o, gt_o,
    X, ST, IDS, SID, GV, GS, CS, CV, YS, YR, XS, RX, LV, LS, LOS, LOR, LFIN,
    xs, xr, cs, cr, ys, yr, ids_s, ids_r, gs_s, gs_r, rs, rr, cvs, cvr, os, orr, los, lor, ready,
):
    WD, R = img.shape
    H = R // 2
    C = R // n_parts
    NH = n_parts // 2
    N_PIECES = R // 128
    PER = C // 128
    KW = 2 * WD
    STEP = 576
    d = lax.axis_index("dp")
    f = lax.axis_index("feat")
    n_cell = n_dp // 2
    c = d // 2
    a = lax.rem(d, 2)
    flip = c // (n_cell // 2)
    role = lax.rem(f + flip, 2)
    other = 1 - f
    c_next = lax.rem(c + 1, n_cell)
    c_last = lax.rem(c + n_cell - 1, n_cell)
    f_next = lax.rem(role + c_next // (n_cell // 2), 2)
    f_last = lax.rem(role + c_last // (n_cell // 2), 2)
    partner = (d, other)
    core = (2 * c + 1 - a, f)
    diag = (2 * c + 1 - a, other)

    def nxt(core_index):
        return (2 * c_next + core_index, f_next)

    def last(core_index):
        return (2 * c_last + core_index, f_last)

    own_at = pl.multiple_of(f * WD, WD)
    oth_at = pl.multiple_of(other * WD, WD)
    own_half, oth_half = pl.ds(own_at, WD), pl.ds(oth_at, WD)
    a_part = pl.ds(pl.multiple_of(a * H, H), H)

    def chunk(j):
        return pl.ds(pl.multiple_of(j * C, C), C) if not isinstance(j, int) else pl.ds(j * C, C)

    def piece(q):
        return pl.ds(pl.multiple_of(q * 128, 128), 128) if not isinstance(q, int) else pl.ds(q * 128, 128)

    def rcopy(src, dst, ssem, rsem, dev):
        return pltpu.make_async_remote_copy(
            src_ref=src, dst_ref=dst, send_sem=ssem, recv_sem=rsem, device_id=dev, device_id_type=MESH
        )

    def got(dst, rsem):
        pltpu.make_async_copy(dst, dst, rsem).wait()

    def sent(src, ssem):
        pltpu.make_async_copy(src, src, ssem).wait()

    barrier = pltpu.get_barrier_semaphore()
    near = (partner, core, diag)

    def arrive(far, senders):
        for dev in (*near, far):
            pl.semaphore_signal(barrier, inc=1, device_id=dev, device_id_type=MESH)

        @pl.when(a != senders)
        def _():
            pl.semaphore_wait(barrier, len(near))
            pl.semaphore_signal(ready, inc=1, device_id=partner, device_id_type=MESH)

        pl.when(a == senders)(lambda: pl.semaphore_wait(ready, 1))

    def neighbours_in():
        pl.semaphore_wait(barrier, len(near) + 2)

    raws = (img, txt)

    def send_raw(kind, slot):
        raw = raws[kind]
        for j in range(n_parts):
            rcopy(raw.at[:, chunk(j)], X.at[slot, own_half, chunk(j)], xs.at[kind, j], xr.at[kind, j], partner).start()

    def raw_sent(kind):
        for j in range(n_parts):
            sent(raws[kind].at[:, chunk(j)], xs.at[kind, j])

    def place(kind, slot):
        def some(i):
            X[slot, pl.ds(pl.multiple_of(own_at + i, STEP), STEP), :] = raws[kind][pl.ds(i, STEP), :]

        by_rows(WD, STEP, some)

    def assemble(kind, slot, j):
        got(X.at[slot, oth_half, chunk(j)], xr.at[kind, j])

    def whole(slot, j):
        return X.at[slot, :, chunk(j)]

    def to_core(slot, j):
        rcopy(whole(slot, j), whole(slot, j), cs.at[slot, j], cr.at[slot, j], core).start()

    def from_core(slot, j):
        got(whole(slot, j), cr.at[slot, j])

    def to_core_sent(slot, j):
        sent(whole(slot, j), cs.at[slot, j])

    def move_own(kind, j, dev):
        rcopy(raws[kind].at[:, chunk(j)], X.at[3, own_half, chunk(j)], ys.at[0, j], yr.at[0, j], dev).start()

    def move(slot, j, dev):
        rcopy(X.at[slot, oth_half, chunk(j)], X.at[3, oth_half, chunk(j)], ys.at[1, j], yr.at[1, j], dev).start()

    def move_sent(kind, slot, j):
        sent(raws[kind].at[:, chunk(j)], ys.at[0, j])
        sent(X.at[slot, oth_half, chunk(j)], ys.at[1, j])

    def moved_in(f_sender):
        for k in range(NH):
            j = a * NH + k
            for n, half in enumerate((f_sender, 1 - f_sender)):
                got(X.at[3, pl.ds(pl.multiple_of(half * WD, WD), WD), chunk(j)], yr.at[n, j])

    def ids_to_core(slot):
        rcopy(IDS.at[slot], IDS.at[slot], ids_s.at[slot], ids_r.at[slot], core).start()

    def ids_move(slot, k, dev):
        rcopy(IDS.at[slot], IDS.at[3], ids_s.at[3 + k], ids_r.at[3], dev).start()

    def ids_of(slot):
        got(IDS.at[slot], ids_r.at[slot])

    def column(s_acc, slot):
        for j in range(n_parts):
            row = IDS[slot, 0:1, chunk(j)]
            SID[s_acc, chunk(j), :] = jnp.transpose(jnp.broadcast_to(row, (128, C)))

    def turned(s_acc, j, image_rows):
        if image_rows and s_acc == 0:
            return pl.ds(0, C)
        return pl.ds(pl.multiple_of(C + j * C, C), C)

    def units(jobs, image_rows, first):
        rights = [X[s_slot, :, chunk(j)] for _, _, _, s_slot, j in jobs]
        lefts = [X[v_slot, :, a_part] for _, v_slot, _, _, _ in jobs]
        if first:
            done = []
            for (_, _, s_acc, s_slot, j), right in zip(jobs, rights):
                if s_slot not in done:
                    ST[turned(s_acc, j, image_rows), :] = jnp.transpose(right)
                    done.append(s_slot)
        scores = [
            jnp.dot(ST[turned(s_acc, j, image_rows), :], left, preferred_element_type=F32)
            for (_, _, s_acc, _, j), left in zip(jobs, lefts)
        ]
        v_sums, s_sums = {}, {}
        for (v, v_slot, s_acc, _, j), right, left, score in zip(jobs, rights, lefts, scores):
            logits = (scale * LOG2E) * score + BIAS * LOG2E
            sid = jnp.concatenate([SID[s_acc, chunk(j), :]] * (H // 128), axis=1)
            same = sid == IDS[v_slot, 0:1, a_part]
            e = jnp.exp2(-jnp.abs(logits))
            den = 1.0 + e
            inv = pl.reciprocal(den, approx=True)
            inv = inv * (2.0 - den * inv)
            z = jnp.where(same, -logits, logits)
            sig = jnp.where(z >= 0, inv, e * inv)
            w = jnp.where(same, -sig, sig).astype(BF16)
            total, prod = jnp.maximum(z, 0.0), e
            if image_rows:
                while total.shape[0] > 8:
                    n = total.shape[0] // 2
                    total = total[:n] + total[n:]
                    prod = join(prod[:n], prod[n:])
                LV[v] += LN2 * total + log1p_of(prod)
            else:
                while total.shape[1] > 128:
                    n = total.shape[1] // 2
                    total = total[:, :n] + total[:, n:]
                    prod = join(prod[:, :n], prod[:, n:])
                LS[0, chunk(j), :] += total
                LS[1, chunk(j), :] = join(LS[1, chunk(j), :], prod)
            v_part = jnp.dot(right, w, preferred_element_type=F32)
            v_sums[v] = v_sums[v] + v_part if v in v_sums else v_part
            s_part_of = lax.dot_general(left, w, (((1,), (1,)), ((), ())), preferred_element_type=F32)
            at = (s_acc, id(j))
            s_sums[at] = ((s_acc, j), s_sums[at][1] + s_part_of if at in s_sums else s_part_of)
        for v, value in v_sums.items():
            GV[v] += value
        for (s_acc, j), value in s_sums.values():
            if first:
                GS[s_acc, :, chunk(j)] = value
            else:
                GS[s_acc, :, chunk(j)] += value

    def rows_at(base, i):
        return pl.ds(pl.multiple_of(base + i, STEP), STEP)

    def staged(b, q):
        return piece(b * (N_PIECES // 2) + q)

    def give(b, q, value, kind, dst, dev):
        def some(i):
            XS[pl.ds(i, STEP), staged(b, q)] = code(scale * value(rows_at(oth_at, i)))

        by_rows(WD, STEP, some)
        rcopy(XS.at[:, staged(b, q)], RX.at[kind, :, piece(dst)], os.at[b, q], orr.at[kind, dst], dev).start()

    def given(b, n):
        def one(q, carry):
            sent(XS.at[:, staged(b, q)], os.at[b, q])
            return carry

        lax.fori_loop(0, n, one, 0)

    def keep(out, q, value, plus=False):
        def some(i):
            mine = scale * value(rows_at(own_at, i))
            out[pl.ds(i, STEP), piece(q)] = out[pl.ds(i, STEP), piece(q)] + mine if plus else mine

        by_rows(WD, STEP, some)

    def taken(out, kind, q, plus):
        got(RX.at[kind, :, piece(q)], orr.at[kind, q])

        def some(i):
            value = decode(RX[kind, pl.ds(i, STEP), piece(q)])
            out[pl.ds(i, STEP), piece(q)] = out[pl.ds(i, STEP), piece(q)] + value if plus else value

        by_rows(WD, STEP, some)

    def taken_from_both(out, kind, plus):
        def one(q):
            taken(out, kind, q, plus)
            taken(out, kind, N_PIECES // 2 + q, plus)

        over(N_PIECES // 2, one)

    def over(n, body):
        def one(q, carry):
            body(q)
            return carry

        lax.fori_loop(0, n, one, 0)

    def turn_back(v, dev):
        def one(q):
            def some(i):
                YS[pl.ds(i, STEP), piece(q)] = code(GV[v, pl.ds(i, STEP), piece(q)])

            by_rows(KW, STEP, some)
            rcopy(YS.at[:, piece(q)], YR.at[:, piece(q)], rs.at[q], rr.at[q], dev).start()

        over(N_PIECES // 2, one)

    def turned_back():
        over(N_PIECES // 2, lambda q: sent(YS.at[:, piece(q)], rs.at[q]))

    def v_value(v, q):
        return lambda rows: GV[v, rows, piece(q)]

    def with_returned(v, q):
        got(YR.at[:, piece(q)], rr.at[q])
        return lambda rows: GV[v, rows, piece(q)] + decode(YR[rows, piece(q)])

    def cv_send(q, value):
        def some(i):
            CV[0, pl.ds(i, STEP), piece(q)] = scale * value(rows_at(own_at, i))

        by_rows(WD, STEP, some)
        rcopy(CV.at[0, :, piece(q)], CV.at[1, :, piece(q)], cvs.at[q], cvr.at[q], core).start()

    def cv_keep(out, base, plus=False):
        def one(q):
            got(CV.at[1, :, piece(q)], cvr.at[q])

            def some(i):
                mine = CV[1, pl.ds(i, STEP), piece(q)]
                at = (pl.ds(i, STEP), piece(base + q))
                out[at] = out[at] + mine if plus else mine

            by_rows(WD, STEP, some)

        over(N_PIECES // 2, one)

    def cv_sent():
        over(N_PIECES // 2, lambda q: sent(CV.at[0, :, piece(q)], cvs.at[q]))

    def s_part(s_acc, j):
        rcopy(GS.at[s_acc, :, chunk(j)], CS.at[:, chunk(j)], gs_s.at[j], gs_r.at[j], core).start()

    def s_part_sent(s_acc):
        for j in range(n_parts):
            sent(GS.at[s_acc, :, chunk(j)], gs_s.at[j])

    def s_home(s_acc, j, out, b, kind, dev):
        got(CS.at[:, chunk(j)], gs_r.at[j])

        def one(i):
            q = j * PER + i

            def value(rows):
                return GS[s_acc, rows, piece(q)] + CS[rows, piece(q)]

            give(b, q, value, kind, q, dev)
            keep(out, q, value)

        over(PER, one)

    def zero():
        def some(i):
            for v in range(3):
                GV[v, pl.ds(i, STEP), :] = jnp.zeros((STEP, H), F32)

        by_rows(KW, STEP, some)
        LV[...] = jnp.zeros_like(LV)

    def zero_rows():
        def some(i):
            LS[:, pl.ds(i, C), :] = jnp.zeros((2, C, 128), F32)

        by_rows(R, C, some)

    def row_of(v):
        return jnp.broadcast_to(jnp.sum(LV[v], axis=0, keepdims=True), (8, H))

    def row_of_s(start):
        col = LN2 * LS[0, start : start + H, :] + log1p_of(LS[1, start : start + H, :])
        row = jnp.sum(jnp.transpose(col), axis=0, keepdims=True)
        return jnp.broadcast_to(row, (8, H))

    mean = 1.0 / float((HOPS + 1) * R)

    def loss_out():
        loss_o[...] = LFIN[0:1, :] * mean

    def loss_to_partner():
        rcopy(LFIN, LFIN, los.at[3], lor.at[3], partner).start()

    def role_0():
        arrive(nxt(0), 0)

        @pl.when(a == 0)
        def _():
            send_raw(1, 1)
            place(0, 0)
            place(1, 1)
            neighbours_in()
            IDS[0] = jnp.broadcast_to(iid[...], (8, R))
            IDS[1] = jnp.broadcast_to(tid[...], (8, R))
            ids_to_core(0)
            ids_to_core(1)
            ids_move(0, 0, last(0))
            ids_move(0, 1, last(1))
            for j in range(n_parts):
                move_own(0, j, last(j // NH))

        @pl.when(a == 1)
        def _():
            send_raw(1, 2)
            send_raw(0, 0)
            IDS[2] = jnp.broadcast_to(tid[...], (8, R))
            ids_to_core(2)
            place(1, 2)

        zero()

        @pl.when(a == 0)
        def _():
            ids_of(2)
            ids_of(3)
            column(0, 2)
            column(1, 1)
            for j in range(n_parts):
                assemble(0, 0, j)
                if j >= NH:
                    to_core(0, j)
                move(0, j, last(j // NH))

        @pl.when(a == 1)
        def _():
            ids_of(0)
            ids_of(1)
            ids_of(3)
            column(0, 2)
            column(1, 1)
            for j in range(n_parts):
                assemble(1, 2, j)
                to_core(2, j)

        @pl.when(a == 1)
        def _():
            for j in range(NH, n_parts):
                from_core(0, j)

        moved_in(f_next)

        def first(j, carry):
            @pl.when(a == 0)
            def _():
                assemble(1, 1, j)
                to_core(1, j)
                from_core(2, j)

            pl.when(a == 1)(lambda: from_core(1, j))
            units([(1, 3, 0, 2, j), (1, 3, 1, 1, j)], True, True)
            pl.when(a == 0)(lambda: s_part(0, j))

            @pl.when((a == 1) & (j > 0))
            def _():
                s_home(0, j - 1, gt_o, 1, 1, partner)

            return carry

        lax.fori_loop(0, n_parts, first, 0)
        turn_back(1, nxt(a))
        pl.when(a == 1)(lambda: s_home(0, n_parts - 1, gt_o, 1, 1, partner))

        def second(i, carry):
            j = 2 * i
            units([(0, 0, 1, 1, j), (0, 0, 1, 1, j + 1)], True, False)

            @pl.when(a == 1)
            def _():
                s_part(1, j)
                s_part(1, j + 1)

            @pl.when((a == 0) & (i > 0))
            def _():
                s_home(1, j - 2, gt_o, 1, 1, partner)
                s_home(1, j - 1, gt_o, 1, 1, partner)

            return carry

        lax.fori_loop(0, NH, second, 0)
        LOS[0] = row_of(0)
        LOS[1] = row_of(1)
        rcopy(LOS.at[1], LOR.at[1 + a], los.at[1], lor.at[1 + a], nxt(0)).start()

        @pl.when(a == 1)
        def _():
            rcopy(LOS.at[0], LOR.at[0], los.at[0], lor.at[0], core).start()

        @pl.when(a == 0)
        def _():
            s_home(1, n_parts - 2, gt_o, 1, 1, partner)
            s_home(1, n_parts - 1, gt_o, 1, 1, partner)

            def one(q):
                value = with_returned(0, q)
                give(0, q, value, 0, q, partner)
                keep(gi_o, q, value)

            over(N_PIECES // 2, one)
            for i in range(3):
                got(LOR.at[i], lor.at[i])
            LFIN[:, 0:H] = LOS[0] + LOR[1]
            LFIN[:, H:R] = LOR[0] + LOR[2]
            loss_to_partner()
            loss_out()
            taken_from_both(gt_o, 1, True)
            cv_keep(gi_o, N_PIECES // 2)
            raw_sent(1)
            for j in range(n_parts):
                to_core_sent(1, j)
                move_sent(0, 0, j)
            for j in range(NH, n_parts):
                to_core_sent(0, j)
            for k in (0, 1, 3, 4):
                sent(IDS.at[0], ids_s.at[k])
            s_part_sent(0)
            sent(LFIN, los.at[3])

        @pl.when(a == 1)
        def _():
            def one(q):
                value = with_returned(0, q)
                give(0, q, value, 0, N_PIECES // 2 + q, diag)
                cv_send(q, value)
                taken(gi_o, 0, 2 * q, False)
                taken(gi_o, 0, 2 * q + 1, False)

            over(N_PIECES // 2, one)
            taken_from_both(gt_o, 1, True)
            got(LFIN, lor.at[3])
            loss_out()
            raw_sent(0)
            raw_sent(1)
            for j in range(n_parts):
                to_core_sent(2, j)
            sent(IDS.at[2], ids_s.at[2])
            s_part_sent(1)
            sent(LOS.at[0], los.at[0])
            cv_sent()

        given(0, N_PIECES // 2)
        given(1, N_PIECES)
        sent(LOS.at[1], los.at[1])
        turned_back()

    def role_1():
        arrive(last(1), 1)

        @pl.when(a == 0)
        def _():
            send_raw(0, 0)
            send_raw(1, 1)
            IDS[1] = jnp.broadcast_to(tid[...], (8, R))
            ids_to_core(1)
            place(1, 1)

        @pl.when(a == 1)
        def _():
            send_raw(1, 2)
            place(1, 2)
            place(0, 0)
            neighbours_in()
            IDS[0] = jnp.broadcast_to(iid[...], (8, R))
            IDS[2] = jnp.broadcast_to(tid[...], (8, R))
            ids_to_core(0)
            ids_to_core(2)
            ids_move(2, 0, nxt(0))
            ids_move(2, 1, nxt(1))
            for j in range(n_parts):
                move_own(1, j, nxt(j // NH))

        zero()
        zero_rows()

        @pl.when(a == 0)
        def _():
            ids_of(0)
            ids_of(2)
            ids_of(3)
            column(0, 0)
            for j in range(n_parts):
                assemble(1, 1, j)
                if j >= NH:
                    to_core(1, j)
            for j in range(NH):
                from_core(2, j)

        @pl.when(a == 1)
        def _():
            ids_of(1)
            ids_of(3)
            column(0, 0)
            for j in range(n_parts):
                assemble(1, 2, j)
                if j < NH:
                    to_core(2, j)
                move(2, j, nxt(j // NH))
            for j in range(NH, n_parts):
                from_core(1, j)

        def step(j, carry):
            @pl.when(a == 1)
            def _():
                assemble(0, 0, j)
                to_core(0, j)

            pl.when(a == 0)(lambda: from_core(0, j))
            units([(0, 2, 0, 0, j), (1, 1, 0, 0, j)], False, True)
            return carry

        lax.fori_loop(0, n_parts, step, 0)

        @pl.when(a == 0)
        def _():
            over(N_PIECES // 2, lambda q: give(1, q, v_value(1, q), 1, q, partner))

        @pl.when(a == 1)
        def _():
            over(N_PIECES // 2, lambda q: give(1, q, v_value(1, q), 1, N_PIECES // 2 + q, diag))

        moved_in(f_last)

        def final(i, carry):
            j = 2 * i
            units([(2, 3, 0, 0, j), (2, 3, 0, 0, j + 1)], False, False)

            @pl.when(a == 0)
            def _():
                s_part(0, j)
                s_part(0, j + 1)

            @pl.when((a == 1) & (i > 0))
            def _():
                s_home(0, j - 2, gi_o, 2, 0, partner)
                s_home(0, j - 1, gi_o, 2, 0, partner)

            return carry

        lax.fori_loop(0, NH, final, 0)
        turn_back(2, last(a))

        @pl.when(a == 0)
        def _():
            over(N_PIECES // 2, lambda q: keep(gt_o, q, v_value(1, q)))
            LOS[0] = row_of_s(0)
            LOS[1] = row_of_s(H)
            for i in range(2):
                rcopy(LOS.at[i], LOR.at[i], los.at[i], lor.at[i], core).start()

            def one(q):
                value = with_returned(0, q)
                give(0, q, value, 1, q, diag)
                cv_send(q, value)
                taken(gt_o, 1, 2 * q, True)
                taken(gt_o, 1, 2 * q + 1, True)

            cv_keep(gt_o, N_PIECES // 2)
            over(N_PIECES // 2, one)
            taken_from_both(gi_o, 0, False)
            got(LFIN, lor.at[3])
            loss_out()
            raw_sent(0)
            raw_sent(1)
            for j in range(NH, n_parts):
                to_core_sent(1, j)
            sent(IDS.at[1], ids_s.at[1])
            s_part_sent(0)
            for i in range(2):
                sent(LOS.at[i], los.at[i])

        @pl.when(a == 1)
        def _():
            s_home(0, n_parts - 2, gi_o, 2, 0, partner)
            s_home(0, n_parts - 1, gi_o, 2, 0, partner)
            over(N_PIECES // 2, lambda q: cv_send(q, v_value(1, q)))
            for i in range(2):
                got(LOR.at[i], lor.at[i])
                LFIN[:, i * H : (i + 1) * H] = row_of_s(i * H) + LOR[i]
            loss_to_partner()
            loss_out()

            def one(q):
                value = with_returned(0, q)
                give(0, q, value, 1, N_PIECES // 2 + q, partner)
                keep(gt_o, N_PIECES // 2 + q, value, plus=True)

            over(N_PIECES, lambda q: taken(gt_o, 1, q, False))
            over(N_PIECES // 2, one)
            cv_keep(gt_o, 0, plus=True)
            raw_sent(1)
            for j in range(n_parts):
                to_core_sent(0, j)
                move_sent(1, 2, j)
            for j in range(NH):
                to_core_sent(2, j)
            for k in (0, 2, 3, 4):
                sent(IDS.at[0], ids_s.at[k])
            given(2, N_PIECES)
            sent(LFIN, los.at[3])

        given(0, N_PIECES // 2)
        given(1, N_PIECES // 2)
        turned_back()
        cv_sent()

    pl.when(role == 0)(role_0)
    pl.when(role == 1)(role_1)


def per_device(n_dp, n_parts, image_emb, text_emb, image_ids, text_ids):
    R, width = image_emb.shape
    H, C = R // 2, R // n_parts
    KW = 2 * width
    scale = TEMPER / math.sqrt(KW)
    ids = [i[None, :] for i in (image_ids, text_ids)]
    dma = pltpu.SemaphoreType.DMA
    vmem = pltpu.VMEM
    scratch = [
        vmem((4, KW, R), BF16),
        vmem((C + R, KW), BF16),
        vmem((4, 8, R), jnp.int32),
        vmem((2, R, 128), jnp.int32),
        vmem((3, KW, H), F32),
        vmem((2, KW, R), F32),
        vmem((KW, R), F32),
        vmem((2, width, H), F32),
        vmem((KW, H), BF16),
        vmem((KW, H), BF16),
        vmem((width, 2 * R), BF16),
        vmem((2, width, R), BF16),
        vmem((2, 8, H), F32),
        vmem((2, R, 128), F32),
        vmem((2, 8, H), F32),
        vmem((3, 8, H), F32),
        vmem((8, R), F32),
        dma((2, n_parts)), dma((2, n_parts)),
        dma((3, n_parts)), dma((3, n_parts)),
        dma((2, n_parts)), dma((2, n_parts)),
        dma((5,)), dma((4,)),
        dma((n_parts,)), dma((n_parts,)),
        dma((R // 256,)), dma((R // 256,)),
        dma((R // 256,)), dma((R // 256,)),
        dma((3, R // 128)), dma((2, R // 128)),
        dma((4,)), dma((4,)),
        pltpu.SemaphoreType.REGULAR,
    ]
    flops = 9 * 2 * H * R * KW
    loss, grad_image, grad_text = pl.pallas_call(
        functools.partial(kernel, n_dp, n_parts, scale),
        out_shape=[
            pltpu.VMEM((1, R), F32),
            pltpu.VMEM((width, R), F32),
            pltpu.VMEM((width, R), F32),
        ],
        in_specs=[pl.BlockSpec(memory_space=vmem)] * 4,
        out_specs=[pl.BlockSpec(memory_space=vmem)] * 3,
        scratch_shapes=scratch,
        compiler_params=pltpu.CompilerParams(
            collective_id=0, has_side_effects=True, vmem_limit_bytes=56 * 2**20
        ),
        cost_estimate=pl.CostEstimate(flops=flops, bytes_accessed=12 * R * width, transcendentals=4 * H * R),
    )(image_emb.T, text_emb.T, *ids)
    return (loss[0], grad_image.T, grad_text.T)


def solution(mesh):
    in_specs = (P("dp", "feat"), P("dp", "feat"), P("dp"), P("dp"))
    out_specs = (P("dp"), P("dp", "feat"), P("dp", "feat"))
    body = functools.partial(per_device, mesh.shape["dp"], 4)
    return jax.shard_map(body, mesh=mesh, in_specs=in_specs, out_specs=out_specs, check_vma=False)
```
